32 devices in a mesh: seq: 8 (over z, y), fsdp: 4 (over x, core).
Axes of the slice: x: 2, y: 2, z: 4, core: 2. Of those that a mesh axis runs over, the one named last changes fastest.
Arguments:
- x_tokens: bfloat16 [5120, 5120], P('seq', 'fsdp'), may hold values from -6 to 6
- w_qkv: bfloat16 [3, 5120, 5120], P(None, 'seq', 'fsdp'), may hold values from -0.078125 to 0.078125
- q_gain: float32 [5120], P('fsdp'), may hold values from 0.5 to 6
- k_gain: float32 [5120], P('fsdp'), may hold values from 0.5 to 6
- head_kind: int32 [40], P('fsdp'), may hold values from 0 to 1, as said below
- block_live: int32 [8, 40, 5, 5], P('seq', 'fsdp'), may hold values from 0 to 1, as said below
Outputs:
- attended: bfloat16 [5120, 5120], P('seq', 'fsdp')
The draws below stay inside these ranges and needn't reach their ends.
Inputs may be any that keep to these rules, and one draw needn't show every extreme that they name: `head_kind`: each aligned block of 10 consecutive heads holds exactly 5 heads labelled 1. block_live[f, h, i, i] is 1 for every frame, head and block i.
All inputs are finite; a program needn't handle non-finite values.
Results may differ from the reference program's by a relative error of at most 0.006.
The reference program's roundings to bfloat16 on the way (of `values`, `sp_weights`, `spatial`, `tm_weights` and `temporal`) count: a program that leaves them out, or rounds other values in their place, can miss the bound.
Values may be sent and summed in bfloat16 or wider, within the bound.
A program may use at most 128 MiB of HBM per device.

```python
import math
import jax
import jax.numpy as jnp
from jax import lax

D = 5120
H = 40
HD = 128
S_POS = 640
BLK = 128
FRAMES = 8
TOKENS = 5120
NB = 5
HEADS_DEV = 10
TEMP_DEV = 5


def spread_gain(key, low_gain, high_gain):
    uniform_part = jax.random.uniform(key, (H * HD,), jnp.float32)
    return jnp.exp(math.log(low_gain) + uniform_part * (math.log(high_gain) - math.log(low_gain)))


def draw_q_gain(key, part):
    key = jax.random.fold_in(key, 11)
    return spread_gain(key, 0.5, 2.5)


def draw_k_gain(key, part):
    key = jax.random.fold_in(key, 17)
    return spread_gain(key, 0.5, 2.5)


def draw_head_kind(key, part):
    key = jax.random.fold_in(key, 23)
    groups = H // HEADS_DEV
    scores = jax.random.randint(key, (groups, HEADS_DEV), 0, 1 << 20) * HEADS_DEV + jnp.arange(HEADS_DEV, dtype=jnp.int32)[None, :]
    head_rank = jnp.argsort(jnp.argsort(scores, axis=1, stable=True), axis=1, stable=True)
    return (head_rank < TEMP_DEV).astype(jnp.int32).reshape(H)


def draw_block_live(key, part):
    key = jax.random.fold_in(key, 37)
    reach_key, roll_key = jax.random.split(key)
    reach_keys = jax.random.randint(reach_key, (FRAMES, 1, 1, 1), 1, NB + 1)
    roll_keys = jax.random.randint(roll_key, (FRAMES, H, NB, NB), 0, NB)
    diagonal = (jnp.arange(NB)[:, None] == jnp.arange(NB)[None, :])[None, None]
    return jnp.logical_or(roll_keys < reach_keys, diagonal).astype(jnp.int32)


def block_levels(rng, dims, shards, smallest, top_value):
    level = 1.0
    for axis_at, parts in shards:
        steps = jax.random.uniform(jax.random.fold_in(jax.random.fold_in(rng, 6), axis_at), (parts,), jnp.float32, smallest / len(shards), top_value / len(shards))
        level = level * jnp.repeat(jnp.exp(steps), dims[axis_at] // parts).reshape((-1,) + (1,) * (len(dims) - 1 - axis_at))
    return level


def bell_draw(key, shape, spread, most, pieces=(), held_as=jnp.bfloat16):
    result = jax.random.normal(key, shape, jnp.float32) * spread
    if len(pieces) > 0:
        result = block_levels(key, shape, pieces, -0.22, 0.18) * result
    return jnp.clip(result, min=-most, max=most).astype(held_as)


def setup_inputs(seed: int = 0) -> dict:
    keys = jax.random.split(jax.random.key(seed), 7)
    return {
        "x_tokens": bell_draw(keys[0], (TOKENS, D), 1.0, 6.0, ((0, 8), (1, 4))),
        "w_qkv": bell_draw(keys[1], (3, D, H * HD), D ** -0.5, 0.078125, ((1, 8), (2, 4))),
        "q_gain": draw_q_gain(jax.random.fold_in(keys[6], 71), 0),
        "k_gain": draw_k_gain(jax.random.fold_in(keys[6], 71), 0),
        "head_kind": draw_head_kind(jax.random.fold_in(keys[6], 71), 0),
        "block_live": draw_block_live(jax.random.fold_in(keys[6], 71), 0),
    }


def softmax_rows(scores):
    row_max = lax.optimization_barrier(jnp.max(scores, axis=-1, keepdims=True))
    expo = jnp.exp(scores - row_max)
    return (expo / lax.optimization_barrier(jnp.sum(expo, axis=-1, keepdims=True))).astype(jnp.bfloat16)

def normalize(raw_rows, gain):
    mean_sq = lax.optimization_barrier(jnp.mean(raw_rows * raw_rows, axis=-1, keepdims=True))
    return (raw_rows * lax.rsqrt(mean_sq + 1e-06) * gain).astype(jnp.bfloat16)

def reference(x_tokens, w_qkv, q_gain, k_gain, head_kind, block_live):
    score_scale = 1.0 / math.sqrt(HD)
    queries = normalize(jnp.dot(x_tokens, w_qkv[0], preferred_element_type=jnp.float32), q_gain)
    keys_n = normalize(jnp.dot(x_tokens, w_qkv[1], preferred_element_type=jnp.float32), k_gain)
    values = jnp.dot(x_tokens, w_qkv[2], preferred_element_type=jnp.float32).astype(jnp.bfloat16)
    grid_shape = (FRAMES, S_POS, H, HD)
    query_grid = queries.reshape(grid_shape)
    key_grid = keys_n.reshape(grid_shape)
    value_grid = values.reshape(grid_shape)

    def spatial_frame(frame_args):
        frame_q, frame_k, frame_v, frame_live = frame_args
        scores = jnp.einsum('qhd,khd->hqk', frame_q.astype(jnp.float32), frame_k.astype(jnp.float32)) * score_scale
        key_mask = jnp.repeat(jnp.repeat(frame_live, BLK, axis=1), BLK, axis=2)
        scores = jnp.where(key_mask > 0, scores, -1e+30)
        sp_weights = softmax_rows(scores)
        return jnp.einsum('hqk,khd->qhd', sp_weights.astype(jnp.float32), frame_v.astype(jnp.float32)).astype(jnp.bfloat16)
    spatial = lax.map(spatial_frame, (query_grid, key_grid, value_grid, block_live))
    scores = jnp.einsum('fphd,gphd->phfg', query_grid.astype(jnp.float32), key_grid.astype(jnp.float32)) * score_scale
    tm_weights = softmax_rows(scores)
    temporal = jnp.einsum('phfg,gphd->fphd', tm_weights.astype(jnp.float32), value_grid.astype(jnp.float32)).astype(jnp.bfloat16)
    is_temporal = (head_kind > 0)[None, None, :, None]
    return jnp.where(is_temporal, temporal, spatial).reshape(TOKENS, H * HD)
```

```python
import math

import jax
import jax.numpy as jnp
from jax import lax
from jax.experimental import pallas as pl
from jax.experimental.pallas import tpu as pltpu
from jax.sharding import PartitionSpec as P

H = 40
HD = 128
BLK = 128


def softmax_rows(scores):
    row_max = jnp.max(scores, axis=-1, keepdims=True)
    expo = jnp.exp(scores - row_max)
    return (expo / jnp.sum(expo, axis=-1, keepdims=True)).astype(jnp.bfloat16)


def spatial_attend(queries, keys_n, values, live_blocks):
    score_scale = 1.0 / math.sqrt(HD)
    scores = (
        jnp.einsum("fqhd,fkhd->fhqk", queries, keys_n, preferred_element_type=jnp.float32)
        * score_scale
    )
    key_mask = jnp.repeat(jnp.repeat(live_blocks, BLK, axis=2), BLK, axis=3)
    scores = jnp.where(key_mask, scores, -1e30)
    sp_weights = softmax_rows(scores)
    return jnp.einsum(
        "fhqk,fkhd->fqhd", sp_weights, values, preferred_element_type=jnp.float32
    ).astype(jnp.bfloat16)


def temporal_attend(triple):
    queries, keys_n, values = triple
    frame_count, single, pos_count, col_width = queries.shape
    head_count = col_width // HD
    grid_shape = (frame_count, pos_count, head_count, HD)
    score_scale = 1.0 / math.sqrt(HD)
    scores = (
        jnp.einsum(
            "fphd,gphd->phfg",
            queries.reshape(grid_shape),
            keys_n.reshape(grid_shape),
            preferred_element_type=jnp.float32,
        )
        * score_scale
    )
    tm_weights = softmax_rows(scores)
    result = jnp.einsum(
        "phfg,gphd->fphd",
        tm_weights,
        values.reshape(grid_shape),
        preferred_element_type=jnp.float32,
    )
    return result.astype(jnp.bfloat16).reshape(frame_count, single, pos_count, col_width)


def shards(x_tokens, w_qkv, q_gain, k_gain, head_kind, block_live):
    full_tokens = lax.all_gather(x_tokens, "fsdp", axis=1, tiled=True)
    tok_rows = full_tokens.shape[0]
    col_width = w_qkv.shape[2]

    def add_rows(shard_rows):
        return jnp.dot(full_tokens, shard_rows, preferred_element_type=jnp.float32)

    q_raw = add_rows(lax.all_gather(w_qkv[0], "seq", axis=0, tiled=True))
    k_raw = add_rows(lax.all_gather(w_qkv[1], "seq", axis=0, tiled=True))
    v_raw = add_rows(lax.all_gather(w_qkv[2], "seq", axis=0, tiled=True))
    q_sq, k_sq = lax.psum((jnp.sum(q_raw * q_raw, axis=1), jnp.sum(k_raw * k_raw, axis=1)), "fsdp")
    total_cols = H * HD
    queries = (q_raw * lax.rsqrt(q_sq[:, None] / total_cols + 1e-06) * q_gain).astype(jnp.bfloat16)
    keys_n = (k_raw * lax.rsqrt(k_sq[:, None] / total_cols + 1e-06) * k_gain).astype(jnp.bfloat16)
    values = v_raw.astype(jnp.bfloat16)
    seq_count = lax.axis_size("seq")
    frames_dev = block_live.shape[0]
    positions = tok_rows // frames_dev
    per_device = positions // seq_count
    head_count = col_width // HD
    live_blocks = block_live > 0

    def to_blocks(columns):
        return columns.reshape(frames_dev, seq_count, per_device, col_width)

    relayed = temporal_attend(
        (
            lax.all_to_all(to_blocks(queries), "seq", split_axis=1, concat_axis=0, tiled=True),
            lax.all_to_all(to_blocks(keys_n), "seq", split_axis=1, concat_axis=0, tiled=True),
            lax.all_to_all(to_blocks(values), "seq", split_axis=1, concat_axis=0, tiled=True),
        )
    )
    returned = lax.all_to_all(relayed, "seq", split_axis=0, concat_axis=1, tiled=True).reshape(
        tok_rows, col_width
    )
    grid_shape = (frames_dev, positions, head_count, HD)
    spatial = spatial_attend(
        queries.reshape(grid_shape),
        keys_n.reshape(grid_shape),
        values.reshape(grid_shape),
        live_blocks,
    )
    is_temporal = jnp.repeat(head_kind > 0, HD)[None, :]
    return jnp.where(is_temporal, returned, spatial.reshape(tok_rows, col_width))

def attend_kernel(role_ref, bias_ref, q_ref, k_ref, v_ref, out_ref):
    head = pl.program_id(0)
    score_scale = 1.0 / math.sqrt(HD)
    slots, quarter, _ = q_ref.shape
    frame_slots = slots // 2
    frame_rows = frame_slots * quarter
    blocks = frame_rows // BLK
    contract_last = (((1,), (1,)), ((), ()))

    def weigh(scores, vals):
        row_max = jnp.max(scores, axis=-1, keepdims=True)
        expo = jnp.exp(scores - row_max)
        weights = (expo * (1.0 / jnp.sum(expo, axis=-1, keepdims=True))).astype(jnp.bfloat16)
        return jnp.dot(weights, vals, preferred_element_type=jnp.float32).astype(jnp.bfloat16)

    @pl.when(role_ref[0] == 1)
    def _():
        for frame in range(2):
            at = pl.ds(frame * frame_slots, frame_slots)
            qs = q_ref[at].reshape(frame_rows, HD)
            ks = k_ref[at].reshape(frame_rows, HD)
            vs = v_ref[at].reshape(frame_rows, HD)
            pieces = []
            for qb in range(blocks):
                scores = (
                    lax.dot_general(
                        qs[qb * BLK : (qb + 1) * BLK],
                        ks,
                        contract_last,
                        preferred_element_type=jnp.float32,
                    )
                    * score_scale
                )
                masked = [
                    scores[:, kb * BLK : (kb + 1) * BLK]
                    + bias_ref[frame, head, qb * blocks + kb]
                    for kb in range(blocks)
                ]
                pieces.append(weigh(jnp.concatenate(masked, axis=1), vs))
            out_ref[at] = jnp.concatenate(pieces, axis=0).reshape(frame_slots, quarter, HD)

    @pl.when(role_ref[0] == 0)
    def _():
        step = 32
        rows = slots * step
        row_pos = lax.broadcasted_iota(jnp.int32, (rows, rows), 0) % step
        col_pos = lax.broadcasted_iota(jnp.int32, (rows, rows), 1) % step
        same = row_pos == col_pos
        for pb in range(quarter // step):
            at = pl.ds(pb * step, step)
            qs = q_ref[:, at].reshape(rows, HD)
            ks = k_ref[:, at].reshape(rows, HD)
            vs = v_ref[:, at].reshape(rows, HD)
            scores = (
                lax.dot_general(qs, ks, contract_last, preferred_element_type=jnp.float32)
                * score_scale
            )
            res = weigh(jnp.where(same, scores, -1e30), vs)
            out_ref[:, at] = res.reshape(slots, step, HD)


def attend(role, bias, queries, keys_n, values):
    slots, quarter, cols = queries.shape
    spec = pl.BlockSpec((slots, quarter, HD), lambda h: (0, 0, h))
    return pl.pallas_call(
        attend_kernel,
        grid=(cols // HD,),
        out_shape=jax.ShapeDtypeStruct(queries.shape, jnp.bfloat16),
        in_specs=[
            pl.BlockSpec(memory_space=pltpu.SMEM),
            pl.BlockSpec(memory_space=pltpu.SMEM),
            spec,
            spec,
            spec,
        ],
        out_specs=spec,
        compiler_params=pltpu.CompilerParams(vmem_limit_bytes=40 * 1024 * 1024),
    )(role, bias, queries, keys_n, values)


def pick_heads(array, heads):
    return jnp.concatenate(
        [lax.dynamic_slice_in_dim(array, head * HD, HD, axis=array.ndim - 1) for head in heads],
        axis=-1,
    )


def along_z(shift, froms):
    return [(2 * z + y, 2 * (z + shift) + y) for z in froms for y in range(2)]


def split_shards(x_tokens, w_qkv, q_gain, k_gain, head_kind, block_live):
    seq_count = lax.axis_size("seq")
    half = seq_count // 2
    me = lax.axis_index("seq")
    z, y = me // 2, me % 2
    is_spatial = me < half
    rows, feats = x_tokens.shape
    quarter = rows // half
    head_count = head_kind.shape[0]
    kept = head_count // 2
    order = jnp.argsort(head_kind, stable=True)
    sp_heads = [order[i] for i in range(kept)]
    tm_heads = [order[kept + i] for i in range(kept)]
    my_heads = [jnp.where(is_spatial, s, t) for s, t in zip(sp_heads, tm_heads)]

    up_half = [(i + half, i) for i in range(half)]
    second = lax.ppermute(x_tokens, "seq", up_half)
    grid = x_tokens.reshape(half, quarter, feats)
    parts = [lax.dynamic_index_in_dim(grid, jnp.maximum(me - half, 0), 0)]
    for r in range(1, seq_count):
        target = (me - r) % seq_count
        block = lax.dynamic_index_in_dim(grid, jnp.maximum(target - half, 0), 0)
        parts.append(
            lax.ppermute(
                block, "seq", [((d + r) % seq_count, d) for d in range(half, seq_count)]
            )
        )
    mine = jnp.where(
        is_spatial,
        jnp.concatenate([grid, second.reshape(grid.shape)], axis=0),
        jnp.concatenate(parts, axis=0),
    ).reshape(2 * rows, feats)
    hf = feats // 2
    mine = jnp.where(y == 0, mine, jnp.concatenate([mine[:, hf:], mine[:, :hf]], axis=1))
    feats_of = lax.all_gather(mine, "fsdp", axis=0, tiled=False)

    w_sp, w_tm = pick_heads(w_qkv, sp_heads), pick_heads(w_qkv, tm_heads)
    swap_y = [(i, i ^ 1) for i in range(seq_count)]
    turn = jnp.where(is_spatial, 1, -1)
    at_z = [z, z + turn, z + 2 * turn, jnp.where(z % 2 == 0, 3, 0)]

    def gather_rows(sp, tm):
        own = jnp.where(is_spatial, sp, tm)
        down = lax.ppermute(sp, "seq", along_z(-1, (1, 2, 3)))
        up = lax.ppermute(tm, "seq", along_z(1, (0, 1, 2)))
        near = jnp.where(is_spatial, down, up)
        down2 = lax.ppermute(down, "seq", along_z(-1, (1, 2)))
        up2 = lax.ppermute(up, "seq", along_z(1, (1, 2)))
        far = jnp.where(is_spatial, down2, up2)
        last = lax.ppermute(
            jnp.where((z == 0) | (z == 3), own, far),
            "seq",
            along_z(1, (0, 2)) + along_z(-1, (1, 3)),
        )
        held = [own, near, far, last]
        return [(piece, lax.ppermute(piece, "seq", swap_y)) for piece in held]

    def project(pieces, count):
        totals = [None] * count
        for z_at, (own, other) in zip(at_z, pieces):
            feat = lax.dynamic_index_in_dim(feats_of, z_at, 0, keepdims=False)
            for part, rows_w in ((feat[:, :hf], own), (feat[:, hf:], other)):
                for i in range(count):
                    term = jnp.dot(part, rows_w[i], preferred_element_type=jnp.float32)
                    totals[i] = term if totals[i] is None else totals[i] + term
        return totals

    q_raw, k_raw = project(gather_rows(w_sp[:2], w_tm[:2]), 2)
    (v_raw,) = project(gather_rows(w_sp[2:], w_tm[2:]), 1)

    sq = jnp.stack([jnp.sum(q_raw * q_raw, axis=1), jnp.sum(k_raw * k_raw, axis=1)])
    blank = jnp.zeros((2, seq_count, rows), jnp.float32)
    sq_sp = sq.reshape(2, 2, rows)
    of_sp = lax.dynamic_update_slice(blank, sq_sp[:, :1], (0, me % half, 0))
    of_sp = lax.dynamic_update_slice(of_sp, sq_sp[:, 1:], (0, me % half + half, 0))
    frame_at = (jnp.arange(seq_count) - me) % seq_count
    pos_at = jnp.maximum(me - half, 0) * quarter
    of_tm = lax.dynamic_update_slice(
        blank, jnp.take(sq.reshape(2, seq_count, quarter), frame_at, axis=1), (0, 0, pos_at)
    )
    sums = lax.psum(jnp.where(is_spatial, of_sp, of_tm), ("seq", "fsdp"))
    sums_sp = jnp.concatenate(
        [
            lax.dynamic_slice(sums, (0, me % half, 0), (2, 1, rows)),
            lax.dynamic_slice(sums, (0, me % half + half, 0), (2, 1, rows)),
        ],
        axis=1,
    ).reshape(2, 2 * rows)
    slot_at = (jnp.arange(seq_count) + me) % seq_count
    sums_tm = jnp.take(
        lax.dynamic_slice(sums, (0, 0, pos_at), (2, seq_count, quarter)), slot_at, axis=1
    ).reshape(2, 2 * rows)
    my_sums = jnp.where(is_spatial, sums_sp, sums_tm)

    def normed(raw, total, gain):
        gains = pick_heads(gain, my_heads)
        scaled = raw * lax.rsqrt(total[:, None] / (H * HD) + 1e-06) * gains
        return scaled.astype(jnp.bfloat16).reshape(seq_count, quarter, kept * HD)

    queries = normed(q_raw, my_sums[0], q_gain)
    keys_n = normed(k_raw, my_sums[1], k_gain)
    values = v_raw.astype(jnp.bfloat16).reshape(seq_count, quarter, kept * HD)

    live = block_live[0]
    live_two = jnp.stack([live, lax.ppermute(live, "seq", up_half)])
    live_two = jnp.take(live_two, order[:kept], axis=1)
    bias = jnp.where(live_two.reshape(2, kept, -1) > 0, 0.0, -1e30).astype(jnp.float32)
    role = is_spatial.astype(jnp.int32).reshape(1)
    done = attend(role, bias, queries, keys_n, values)

    back = lax.ppermute(done[half:], "seq", [(i, i + half) for i in range(half)])
    spatial = jnp.where(is_spatial, done[:half], back).reshape(rows, kept * HD)
    came = [done[:1]]
    for r in range(1, seq_count):
        came.append(
            lax.ppermute(
                done[r : r + 1], "seq", [(s, (s + r) % seq_count) for s in range(half, seq_count)]
            )
        )
    came = jnp.concatenate(came, axis=0)
    came_at = (me - half - jnp.arange(half)) % seq_count
    temporal = jnp.take(came, came_at, axis=0).reshape(rows, kept * HD)
    both = jnp.concatenate([spatial, temporal], axis=1)
    place = jnp.argsort(order)
    return pick_heads(both, [place[h] for h in range(head_count)])


def solution(mesh):
    placed = (
        P("seq", "fsdp"),
        P(None, "seq", "fsdp"),
        P("fsdp"),
        P("fsdp"),
        P("fsdp"),
        P("seq", "fsdp", None, None),
    )

    def chosen(x_tokens, w_qkv, q_gain, k_gain, head_kind, block_live):
        fits = (
            mesh.shape["seq"] == 8
            and head_kind.shape[0] == 10
            and block_live.shape[0] == 1
            and x_tokens.shape[1] * mesh.shape["fsdp"] == w_qkv.shape[1] * mesh.shape["seq"]
            and mesh.shape["fsdp"] == 4
        )
        body = split_shards if fits else shards
        return body(x_tokens, w_qkv, q_gain, k_gain, head_kind, block_live)

    return jax.shard_map(
        chosen, mesh=mesh, in_specs=placed, out_specs=P("seq", "fsdp"), check_vma=False
    )
```

```python
import math

import jax
import jax.numpy as jnp
from jax import lax
from jax.experimental import pallas as pl
from jax.experimental.pallas import tpu as pltpu
from jax.sharding import PartitionSpec as P

H = 40
HD = 128
BLK = 128


def softmax_rows(scores):
    row_max = jnp.max(scores, axis=-1, keepdims=True)
    expo = jnp.exp(scores - row_max)
    return (expo / jnp.sum(expo, axis=-1, keepdims=True)).astype(jnp.bfloat16)


def spatial_attend(queries, keys_n, values, live_blocks):
    score_scale = 1.0 / math.sqrt(HD)
    scores = (
        jnp.einsum("fqhd,fkhd->fhqk", queries, keys_n, preferred_element_type=jnp.float32)
        * score_scale
    )
    key_mask = jnp.repeat(jnp.repeat(live_blocks, BLK, axis=2), BLK, axis=3)
    scores = jnp.where(key_mask, scores, -1e30)
    sp_weights = softmax_rows(scores)
    return jnp.einsum(
        "fhqk,fkhd->fqhd", sp_weights, values, preferred_element_type=jnp.float32
    ).astype(jnp.bfloat16)


def temporal_attend(triple):
    queries, keys_n, values = triple
    frame_count, single, pos_count, col_width = queries.shape
    head_count = col_width // HD
    grid_shape = (frame_count, pos_count, head_count, HD)
    score_scale = 1.0 / math.sqrt(HD)
    scores = (
        jnp.einsum(
            "fphd,gphd->phfg",
            queries.reshape(grid_shape),
            keys_n.reshape(grid_shape),
            preferred_element_type=jnp.float32,
        )
        * score_scale
    )
    tm_weights = softmax_rows(scores)
    result = jnp.einsum(
        "phfg,gphd->fphd",
        tm_weights,
        values.reshape(grid_shape),
        preferred_element_type=jnp.float32,
    )
    return result.astype(jnp.bfloat16).reshape(frame_count, single, pos_count, col_width)


def shards(x_tokens, w_qkv, q_gain, k_gain, head_kind, block_live):
    full_tokens = lax.all_gather(x_tokens, "fsdp", axis=1, tiled=True)
    tok_rows = full_tokens.shape[0]
    col_width = w_qkv.shape[2]

    def add_rows(shard_rows):
        return jnp.dot(full_tokens, shard_rows, preferred_element_type=jnp.float32)

    q_raw = add_rows(lax.all_gather(w_qkv[0], "seq", axis=0, tiled=True))
    k_raw = add_rows(lax.all_gather(w_qkv[1], "seq", axis=0, tiled=True))
    v_raw = add_rows(lax.all_gather(w_qkv[2], "seq", axis=0, tiled=True))
    q_sq, k_sq = lax.psum((jnp.sum(q_raw * q_raw, axis=1), jnp.sum(k_raw * k_raw, axis=1)), "fsdp")
    total_cols = H * HD
    queries = (q_raw * lax.rsqrt(q_sq[:, None] / total_cols + 1e-06) * q_gain).astype(jnp.bfloat16)
    keys_n = (k_raw * lax.rsqrt(k_sq[:, None] / total_cols + 1e-06) * k_gain).astype(jnp.bfloat16)
    values = v_raw.astype(jnp.bfloat16)
    seq_count = lax.axis_size("seq")
    frames_dev = block_live.shape[0]
    positions = tok_rows // frames_dev
    per_device = positions // seq_count
    head_count = col_width // HD
    live_blocks = block_live > 0

    def to_blocks(columns):
        return columns.reshape(frames_dev, seq_count, per_device, col_width)

    relayed = temporal_attend(
        (
            lax.all_to_all(to_blocks(queries), "seq", split_axis=1, concat_axis=0, tiled=True),
            lax.all_to_all(to_blocks(keys_n), "seq", split_axis=1, concat_axis=0, tiled=True),
            lax.all_to_all(to_blocks(values), "seq", split_axis=1, concat_axis=0, tiled=True),
        )
    )
    returned = lax.all_to_all(relayed, "seq", split_axis=0, concat_axis=1, tiled=True).reshape(
        tok_rows, col_width
    )
    grid_shape = (frames_dev, positions, head_count, HD)
    spatial = spatial_attend(
        queries.reshape(grid_shape),
        keys_n.reshape(grid_shape),
        values.reshape(grid_shape),
        live_blocks,
    )
    is_temporal = jnp.repeat(head_kind > 0, HD)[None, :]
    return jnp.where(is_temporal, returned, spatial.reshape(tok_rows, col_width))

def attend_kernel(role_ref, bias_ref, q_ref, k_ref, v_ref, out_ref):
    head = pl.program_id(0)
    score_scale = 1.0 / math.sqrt(HD)
    slots, quarter, _ = q_ref.shape
    frame_slots = slots // 2
    frame_rows = frame_slots * quarter
    blocks = frame_rows // BLK
    contract_last = (((1,), (1,)), ((), ()))

    def weigh(scores, vals):
        row_max = jnp.max(scores, axis=-1, keepdims=True)
        expo = jnp.exp(scores - row_max)
        weights = (expo * (1.0 / jnp.sum(expo, axis=-1, keepdims=True))).astype(jnp.bfloat16)
        return jnp.dot(weights, vals, preferred_element_type=jnp.float32).astype(jnp.bfloat16)

    @pl.when(role_ref[0] == 1)
    def _():
        for frame in range(2):
            at = pl.ds(frame * frame_slots, frame_slots)
            qs = q_ref[at].reshape(frame_rows, HD)
            ks = k_ref[at].reshape(frame_rows, HD)
            vs = v_ref[at].reshape(frame_rows, HD)
            pieces = []
            for qb in range(blocks):
                scores = (
                    lax.dot_general(
                        qs[qb * BLK : (qb + 1) * BLK],
                        ks,
                        contract_last,
                        preferred_element_type=jnp.float32,
                    )
                    * score_scale
                )
                masked = [
                    scores[:, kb * BLK : (kb + 1) * BLK]
                    + bias_ref[frame, head, qb * blocks + kb]
                    for kb in range(blocks)
                ]
                pieces.append(weigh(jnp.concatenate(masked, axis=1), vs))
            out_ref[at] = jnp.concatenate(pieces, axis=0).reshape(frame_slots, quarter, HD)

    @pl.when(role_ref[0] == 0)
    def _():
        step = 32
        rows = slots * step
        row_pos = lax.broadcasted_iota(jnp.int32, (rows, rows), 0) % step
        col_pos = lax.broadcasted_iota(jnp.int32, (rows, rows), 1) % step
        same = row_pos == col_pos
        for pb in range(quarter // step):
            at = pl.ds(pb * step, step)
            qs = q_ref[:, at].reshape(rows, HD)
            ks = k_ref[:, at].reshape(rows, HD)
            vs = v_ref[:, at].reshape(rows, HD)
            scores = (
                lax.dot_general(qs, ks, contract_last, preferred_element_type=jnp.float32)
                * score_scale
            )
            res = weigh(jnp.where(same, scores, -1e30), vs)
            out_ref[:, at] = res.reshape(slots, step, HD)


def attend(role, bias, queries, keys_n, values):
    slots, quarter, cols = queries.shape
    spec = pl.BlockSpec((slots, quarter, HD), lambda h: (0, 0, h))
    return pl.pallas_call(
        attend_kernel,
        grid=(cols // HD,),
        out_shape=jax.ShapeDtypeStruct(queries.shape, jnp.bfloat16),
        in_specs=[
            pl.BlockSpec(memory_space=pltpu.SMEM),
            pl.BlockSpec(memory_space=pltpu.SMEM),
            spec,
            spec,
            spec,
        ],
        out_specs=spec,
        compiler_params=pltpu.CompilerParams(vmem_limit_bytes=40 * 1024 * 1024),
    )(role, bias, queries, keys_n, values)


def spread_kernel(
    x_ref, own_ref, oth_ref, xg_ref, wg_ref, relay_ref,
    x_send, x_recv, near_send, near_recv, core_send, core_recv, pass_send, pass_recv,
    mate_send, mate_recv, cross_send, relay_recv, fwd_send, a1_send, a1_recv, a2_send, a2_recv,
    y_send, y_recv, local_sem,
):
    me, fs = lax.axis_index("seq"), lax.axis_index("fsdp")
    quarter, feats = x_ref.shape[1:]
    kinds = own_ref.shape[0]
    half = 4
    z, y = me // 2, me % 2
    mate = (z + 1 - 2 * (z % 2)) * 2 + y
    side = z // 2
    a1 = (2 - side) * 2 + y
    a2 = (3 - 3 * side) * 2 + y
    other_y = z * 2 + 1 - y
    inner = (z == 1) | (z == 2)
    outer = (z == 0) | (z == 3)
    is_spatial = me < half
    is_temporal = me >= half
    sib = fs + 1 - 2 * (fs % 2)
    across = (fs + 2) % 4

    barrier = pltpu.get_barrier_semaphore()
    for r in range(1, 8):
        pl.semaphore_signal(
            barrier, inc=1, device_id=((me + r) % 8, fs), device_id_type=pl.DeviceIdType.MESH
        )
    for f in (sib, across):
        pl.semaphore_signal(barrier, inc=1, device_id=(me, f), device_id_type=pl.DeviceIdType.MESH)
    pl.semaphore_wait(barrier, 9)

    def remote(src, dst, send, recv, seq, fsdp):
        return pltpu.make_async_remote_copy(
            src_ref=src, dst_ref=dst, send_sem=send, recv_sem=recv,
            device_id=(seq, fsdp), device_id_type=pl.DeviceIdType.MESH,
        )

    def x_cols(f):
        return pl.ds(pl.multiple_of(f * feats, 128), feats)

    def slot(r, f):
        return xg_ref.at[r, :, x_cols(f)]

    def to_temporal(j):
        target = half + j
        r = (me + 8 - target) % 8
        return remote(x_ref.at[j], slot(r, fs), x_send.at[j], x_recv.at[r], target, fs)

    def to_spatial(j):
        target = (me + half) % 8
        return remote(
            x_ref.at[j], slot(half + j, fs), x_send.at[half + j], x_recv.at[half + j], target, fs
        )

    def keep_spatial(j):
        return pltpu.make_async_copy(x_ref.at[j], slot(j, fs), local_sem.at[kinds + j])

    def keep_temporal():
        return pltpu.make_async_copy(x_ref.at[me % half], slot(0, fs), local_sem.at[kinds])

    for j in range(half):
        @pl.when(me != half + j)
        def _():
            to_temporal(j).start()

        @pl.when(is_temporal)
        def _():
            to_spatial(j).start()

        @pl.when(is_spatial)
        def _():
            keep_spatial(j).start()

    @pl.when(is_temporal)
    def _():
        keep_temporal().start()

    def mate_copy(i):
        return remote(own_ref.at[i], wg_ref.at[i, me], mate_send.at[i], mate_recv.at[i], mate, fs)

    def relay_copy(i):
        return remote(oth_ref.at[i], relay_ref.at[i], cross_send.at[i], relay_recv.at[i], mate, fs)

    def cross_copy(i):
        return remote(oth_ref.at[i], wg_ref.at[i, me], cross_send.at[i], a1_recv.at[i], a1, fs)

    def fwd_copy(i):
        return remote(relay_ref.at[i], wg_ref.at[i, mate], fwd_send.at[i], a2_recv.at[i], a1, fs)

    def a1_copy(i):
        at = wg_ref.at[i, a1]
        return remote(at, at, a1_send.at[i], a1_recv.at[i], mate, fs)

    def a2_copy(i):
        at = wg_ref.at[i, a2]
        return remote(at, at, a2_send.at[i], a2_recv.at[i], mate, fs)

    def y_copy(i, k):
        row = (me, mate, a1, a2)[k]
        src = own_ref.at[i] if k == 0 else wg_ref.at[i, row]
        return remote(src, wg_ref.at[i, row], y_send.at[i, k], y_recv.at[i, k], other_y, fs)

    def keep_w(i):
        return pltpu.make_async_copy(own_ref.at[i], wg_ref.at[i, me], local_sem.at[i])

    for i in range(kinds):
        mate_copy(i).start()

        @pl.when(outer)
        def _():
            relay_copy(i).start()

        @pl.when(inner)
        def _():
            cross_copy(i).start()

        y_copy(i, 0).start()
        keep_w(i).start()

    def near_copy(r):
        return remote(slot(r, fs), slot(r, fs), near_send.at[r], near_recv.at[r], me, across)

    def core_copy(r):
        return remote(slot(r, fs), slot(r, fs), core_send.at[r], core_recv.at[r], me, sib)

    def pass_copy(r):
        at = slot(r, across)
        return remote(at, at, pass_send.at[r], pass_recv.at[r], me, sib)

    def x_arrived(r):
        remote(x_ref.at[0], slot(r, fs), x_send.at[0], x_recv.at[r], me, across).wait_recv()

    for r in range(8):
        if r == 0:
            @pl.when(is_temporal)
            def _():
                keep_temporal().wait()
        else:
            @pl.when(is_temporal)
            def _():
                x_arrived(r)
        if r < half:
            @pl.when(is_spatial)
            def _():
                keep_spatial(r).wait()
        else:
            @pl.when(is_spatial)
            def _():
                x_arrived(r)
        near_copy(r).start()
        core_copy(r).start()

    for i in range(kinds):
        mate_copy(i).wait_recv()
        y_copy(i, 1).start()

        @pl.when(inner)
        def _():
            relay_copy(i).wait_recv()
            fwd_copy(i).start()

        a1_copy(i).wait_recv()

        @pl.when(inner)
        def _():
            a1_copy(i).start()

        y_copy(i, 2).start()

    for r in range(8):
        remote(
            slot(r, across), slot(r, across), near_send.at[r], near_recv.at[r], me, across
        ).wait_recv()
        pass_copy(r).start()

    for i in range(kinds):
        a2_copy(i).wait_recv()

        @pl.when(inner)
        def _():
            a2_copy(i).start()

        y_copy(i, 3).start()

    for r in range(8):
        core_copy(r).wait_recv()
        pass_copy(r).wait_recv()
        near_copy(r).wait_send()
        core_copy(r).wait_send()
        pass_copy(r).wait_send()
    for j in range(half):
        @pl.when(me != half + j)
        def _():
            to_temporal(j).wait_send()

        @pl.when(is_temporal)
        def _():
            to_spatial(j).wait_send()

    for i in range(kinds):
        keep_w(i).wait()
        mate_copy(i).wait_send()
        cross_copy(i).wait_send()

        @pl.when(inner)
        def _():
            fwd_copy(i).wait_send()
            a1_copy(i).wait_send()
            a2_copy(i).wait_send()

        for k in range(4):
            y_copy(i, k).wait()


def spread(x_quarters, w_own, w_oth, seq_count, fsdp_count):
    half, quarter, feats = x_quarters.shape
    kinds, rows, cols = w_own.shape
    dma = pltpu.SemaphoreType.DMA
    any_spec = pl.BlockSpec(memory_space=pl.ANY)
    sent = jnp.bfloat16
    return pl.pallas_call(
        spread_kernel,
        out_shape=[
            jax.ShapeDtypeStruct((seq_count, quarter, feats * fsdp_count), sent),
            jax.ShapeDtypeStruct((kinds, seq_count, rows, cols), sent),
            jax.ShapeDtypeStruct((kinds, rows, cols), sent),
        ],
        in_specs=[any_spec] * 3,
        out_specs=[any_spec] * 3,
        scratch_shapes=[dma((8,))] * 8
        + [dma((kinds,))] * 9
        + [dma((kinds, 4)), dma((kinds, 4)), dma((kinds + half,))],
        compiler_params=pltpu.CompilerParams(
            collective_id=0, has_side_effects=True, vmem_limit_bytes=32 * 1024 * 1024
        ),
    )(x_quarters, w_own, w_oth)


def pick_heads(array, heads):
    return jnp.concatenate(
        [lax.dynamic_slice_in_dim(array, head * HD, HD, axis=array.ndim - 1) for head in heads],
        axis=-1,
    )


def split_shards(x_tokens, w_qkv, q_gain, k_gain, head_kind, block_live):
    seq_count = lax.axis_size("seq")
    half = seq_count // 2
    me = lax.axis_index("seq")
    z, y = me // 2, me % 2
    is_spatial = me < half
    rows, feats = x_tokens.shape
    quarter = rows // half
    head_count = head_kind.shape[0]
    kept = head_count // 2
    order = jnp.argsort(head_kind, stable=True)
    sp_heads = [order[i] for i in range(kept)]
    tm_heads = [order[kept + i] for i in range(kept)]
    my_heads = [jnp.where(is_spatial, s, t) for s, t in zip(sp_heads, tm_heads)]

    other_heads = [jnp.where(is_spatial, t, s) for s, t in zip(sp_heads, tm_heads)]

    tokens, weights, _ = spread(
        x_tokens.reshape(half, quarter, feats),
        pick_heads(w_qkv, my_heads),
        pick_heads(w_qkv, other_heads),
        seq_count,
        lax.axis_size("fsdp"),
    )
    tokens = tokens.reshape(2 * rows, -1)
    weights = weights.reshape(weights.shape[0], -1, kept * HD)
    q_raw, k_raw, v_raw = [
        jnp.dot(tokens, weights[i], preferred_element_type=jnp.float32) for i in range(3)
    ]

    sq = jnp.stack([jnp.sum(q_raw * q_raw, axis=1), jnp.sum(k_raw * k_raw, axis=1)])
    sums = lax.all_gather(lax.psum(sq, "fsdp"), "seq", axis=0, tiled=False)
    of_sp = sums[:half].reshape(half, 2, 2, rows).transpose(1, 2, 0, 3)
    of_sp = of_sp.reshape(2, seq_count, rows)
    of_tm = sums[half:].reshape(half, 2, seq_count, quarter).transpose(1, 2, 0, 3)
    of_tm = jnp.stack(
        [
            jnp.take(of_tm[:, :, q], (jnp.arange(seq_count) - half - q) % seq_count, axis=1)
            for q in range(half)
        ],
        axis=2,
    ).reshape(2, seq_count, rows)
    sums = of_sp + of_tm
    sums_sp = jnp.take(sums, me % half + jnp.arange(2) * half, axis=1).reshape(2, 2 * rows)
    pos_at = jnp.maximum(me - half, 0) * quarter
    slot_at = (jnp.arange(seq_count) + me) % seq_count
    sums_tm = jnp.take(
        lax.dynamic_slice(sums, (0, 0, pos_at), (2, seq_count, quarter)), slot_at, axis=1
    ).reshape(2, 2 * rows)
    my_sums = jnp.where(is_spatial, sums_sp, sums_tm)

    def normed(raw, total, gain):
        gains = pick_heads(gain, my_heads)
        scaled = raw * lax.rsqrt(total[:, None] / (H * HD) + 1e-06) * gains
        return scaled.astype(jnp.bfloat16).reshape(seq_count, quarter, kept * HD)

    queries = normed(q_raw, my_sums[0], q_gain)
    keys_n = normed(k_raw, my_sums[1], k_gain)
    values = v_raw.astype(jnp.bfloat16).reshape(seq_count, quarter, kept * HD)

    up_half = [(i + half, i) for i in range(half)]
    live = block_live[0]
    live_two = jnp.stack([live, lax.ppermute(live, "seq", up_half)])
    live_two = jnp.take(live_two, order[:kept], axis=1)
    bias = jnp.where(live_two.reshape(2, kept, -1) > 0, 0.0, -1e30).astype(jnp.float32)
    role = is_spatial.astype(jnp.int32).reshape(1)
    done = attend(role, bias, queries, keys_n, values)

    back = lax.ppermute(done[half:], "seq", [(i, i + half) for i in range(half)])
    spatial = jnp.where(is_spatial, done[:half], back).reshape(rows, kept * HD)
    came = [done[:1]]
    for r in range(1, seq_count):
        came.append(
            lax.ppermute(
                done[r : r + 1], "seq", [(s, (s + r) % seq_count) for s in range(half, seq_count)]
            )
        )
    came = jnp.concatenate(came, axis=0)
    came_at = (me - half - jnp.arange(half)) % seq_count
    temporal = jnp.take(came, came_at, axis=0).reshape(rows, kept * HD)
    both = jnp.concatenate([spatial, temporal], axis=1)
    place = jnp.argsort(order)
    return pick_heads(both, [place[h] for h in range(head_count)])


def solution(mesh):
    placed = (
        P("seq", "fsdp"),
        P(None, "seq", "fsdp"),
        P("fsdp"),
        P("fsdp"),
        P("fsdp"),
        P("seq", "fsdp", None, None),
    )

    def chosen(x_tokens, w_qkv, q_gain, k_gain, head_kind, block_live):
        fits = (
            mesh.shape["seq"] == 8
            and head_kind.shape[0] == 10
            and block_live.shape[0] == 1
            and x_tokens.shape[1] * mesh.shape["fsdp"] == w_qkv.shape[1] * mesh.shape["seq"]
            and mesh.shape["fsdp"] == 4
        )
        body = split_shards if fits else shards
        return body(x_tokens, w_qkv, q_gain, k_gain, head_kind, block_live)

    return jax.shard_map(
        chosen, mesh=mesh, in_specs=placed, out_specs=P("seq", "fsdp"), check_vma=False
    )
```

```python
import math

import jax
import jax.numpy as jnp
from jax import lax
from jax.experimental import pallas as pl
from jax.experimental.pallas import tpu as pltpu
from jax.sharding import PartitionSpec as P

H = 40
HD = 128
BLK = 128


def softmax_rows(scores):
    row_max = jnp.max(scores, axis=-1, keepdims=True)
    expo = jnp.exp(scores - row_max)
    return (expo / jnp.sum(expo, axis=-1, keepdims=True)).astype(jnp.bfloat16)


def spatial_attend(queries, keys_n, values, live_blocks):
    score_scale = 1.0 / math.sqrt(HD)
    scores = (
        jnp.einsum("fqhd,fkhd->fhqk", queries, keys_n, preferred_element_type=jnp.float32)
        * score_scale
    )
    key_mask = jnp.repeat(jnp.repeat(live_blocks, BLK, axis=2), BLK, axis=3)
    scores = jnp.where(key_mask, scores, -1e30)
    sp_weights = softmax_rows(scores)
    return jnp.einsum(
        "fhqk,fkhd->fqhd", sp_weights, values, preferred_element_type=jnp.float32
    ).astype(jnp.bfloat16)


def temporal_attend(triple):
    queries, keys_n, values = triple
    frame_count, single, pos_count, col_width = queries.shape
    head_count = col_width // HD
    grid_shape = (frame_count, pos_count, head_count, HD)
    score_scale = 1.0 / math.sqrt(HD)
    scores = (
        jnp.einsum(
            "fphd,gphd->phfg",
            queries.reshape(grid_shape),
            keys_n.reshape(grid_shape),
            preferred_element_type=jnp.float32,
        )
        * score_scale
    )
    tm_weights = softmax_rows(scores)
    result = jnp.einsum(
        "phfg,gphd->fphd",
        tm_weights,
        values.reshape(grid_shape),
        preferred_element_type=jnp.float32,
    )
    return result.astype(jnp.bfloat16).reshape(frame_count, single, pos_count, col_width)


def shards(x_tokens, w_qkv, q_gain, k_gain, head_kind, block_live):
    full_tokens = lax.all_gather(x_tokens, "fsdp", axis=1, tiled=True)
    tok_rows = full_tokens.shape[0]
    col_width = w_qkv.shape[2]

    def add_rows(shard_rows):
        return jnp.dot(full_tokens, shard_rows, preferred_element_type=jnp.float32)

    q_raw = add_rows(lax.all_gather(w_qkv[0], "seq", axis=0, tiled=True))
    k_raw = add_rows(lax.all_gather(w_qkv[1], "seq", axis=0, tiled=True))
    v_raw = add_rows(lax.all_gather(w_qkv[2], "seq", axis=0, tiled=True))
    q_sq, k_sq = lax.psum((jnp.sum(q_raw * q_raw, axis=1), jnp.sum(k_raw * k_raw, axis=1)), "fsdp")
    total_cols = H * HD
    queries = (q_raw * lax.rsqrt(q_sq[:, None] / total_cols + 1e-06) * q_gain).astype(jnp.bfloat16)
    keys_n = (k_raw * lax.rsqrt(k_sq[:, None] / total_cols + 1e-06) * k_gain).astype(jnp.bfloat16)
    values = v_raw.astype(jnp.bfloat16)
    seq_count = lax.axis_size("seq")
    frames_dev = block_live.shape[0]
    positions = tok_rows // frames_dev
    per_device = positions // seq_count
    head_count = col_width // HD
    live_blocks = block_live > 0

    def to_blocks(columns):
        return columns.reshape(frames_dev, seq_count, per_device, col_width)

    relayed = temporal_attend(
        (
            lax.all_to_all(to_blocks(queries), "seq", split_axis=1, concat_axis=0, tiled=True),
            lax.all_to_all(to_blocks(keys_n), "seq", split_axis=1, concat_axis=0, tiled=True),
            lax.all_to_all(to_blocks(values), "seq", split_axis=1, concat_axis=0, tiled=True),
        )
    )
    returned = lax.all_to_all(relayed, "seq", split_axis=0, concat_axis=1, tiled=True).reshape(
        tok_rows, col_width
    )
    grid_shape = (frames_dev, positions, head_count, HD)
    spatial = spatial_attend(
        queries.reshape(grid_shape),
        keys_n.reshape(grid_shape),
        values.reshape(grid_shape),
        live_blocks,
    )
    is_temporal = jnp.repeat(head_kind > 0, HD)[None, :]
    return jnp.where(is_temporal, returned, spatial.reshape(tok_rows, col_width))

def attend_kernel(role_ref, bias_ref, q_ref, k_ref, v_ref, out_ref):
    head = pl.program_id(0)
    score_scale = 1.0 / math.sqrt(HD)
    slots, quarter, _ = q_ref.shape
    frame_slots = slots // 2
    frame_rows = frame_slots * quarter
    blocks = frame_rows // BLK
    contract_last = (((1,), (1,)), ((), ()))

    def weigh(scores, vals):
        row_max = jnp.max(scores, axis=-1, keepdims=True)
        expo = jnp.exp(scores - row_max)
        weights = (expo * (1.0 / jnp.sum(expo, axis=-1, keepdims=True))).astype(jnp.bfloat16)
        return jnp.dot(weights, vals, preferred_element_type=jnp.float32).astype(jnp.bfloat16)

    @pl.when(role_ref[0] == 1)
    def _():
        for frame in range(2):
            at = pl.ds(frame * frame_slots, frame_slots)
            qs = q_ref[at].reshape(frame_rows, HD)
            ks = k_ref[at].reshape(frame_rows, HD)
            vs = v_ref[at].reshape(frame_rows, HD)
            pieces = []
            for qb in range(blocks):
                scores = (
                    lax.dot_general(
                        qs[qb * BLK : (qb + 1) * BLK],
                        ks,
                        contract_last,
                        preferred_element_type=jnp.float32,
                    )
                    * score_scale
                )
                masked = [
                    scores[:, kb * BLK : (kb + 1) * BLK]
                    + bias_ref[frame, head, qb * blocks + kb]
                    for kb in range(blocks)
                ]
                pieces.append(weigh(jnp.concatenate(masked, axis=1), vs))
            out_ref[at] = jnp.concatenate(pieces, axis=0).reshape(frame_slots, quarter, HD)

    @pl.when(role_ref[0] == 0)
    def _():
        step = 32
        rows = slots * step
        row_pos = lax.broadcasted_iota(jnp.int32, (rows, rows), 0) % step
        col_pos = lax.broadcasted_iota(jnp.int32, (rows, rows), 1) % step
        same = row_pos == col_pos
        for pb in range(quarter // step):
            at = pl.ds(pb * step, step)
            qs = q_ref[:, at].reshape(rows, HD)
            ks = k_ref[:, at].reshape(rows, HD)
            vs = v_ref[:, at].reshape(rows, HD)
            scores = (
                lax.dot_general(qs, ks, contract_last, preferred_element_type=jnp.float32)
                * score_scale
            )
            res = weigh(jnp.where(same, scores, -1e30), vs)
            out_ref[:, at] = res.reshape(slots, step, HD)


def attend(role, bias, queries, keys_n, values):
    slots, quarter, cols = queries.shape
    spec = pl.BlockSpec((slots, quarter, HD), lambda h: (0, 0, h))
    return pl.pallas_call(
        attend_kernel,
        grid=(cols // HD,),
        out_shape=jax.ShapeDtypeStruct(queries.shape, jnp.bfloat16),
        in_specs=[
            pl.BlockSpec(memory_space=pltpu.SMEM),
            pl.BlockSpec(memory_space=pltpu.SMEM),
            spec,
            spec,
            spec,
        ],
        out_specs=spec,
        compiler_params=pltpu.CompilerParams(vmem_limit_bytes=40 * 1024 * 1024),
    )(role, bias, queries, keys_n, values)


def project_kernel(
    x_ref, own_ref, oth_ref, gain_ref, q_ref, k_ref, v_ref,
    xg_ref, wg_ref, relay_ref, total, sq, sq_in, sq_out,
    x_send, x_recv, near_send, near_recv, core_send, core_recv, pass_send, pass_recv,
    cast_send, cast_recv, mate_send, mate_recv, cross_send, relay_recv, fwd_send, a1_send, a1_recv,
    a2_send, a2_recv, y_send, y_recv, sum_send, sum_recv, local_sem,
):
    me, fs = lax.axis_index("seq"), lax.axis_index("fsdp")
    quarter, feats = x_ref.shape[1:]
    kinds = own_ref.shape[0]
    half = 4
    z, y = me // 2, me % 2
    mate = (z + 1 - 2 * (z % 2)) * 2 + y
    side = z // 2
    a1 = (2 - side) * 2 + y
    a2 = (3 - 3 * side) * 2 + y
    other_y = z * 2 + 1 - y
    inner = (z == 1) | (z == 2)
    outer = (z == 0) | (z == 3)
    is_spatial = me < half
    is_temporal = me >= half
    sib = fs + 1 - 2 * (fs % 2)
    across = (fs + 2) % 4

    barrier = pltpu.get_barrier_semaphore()
    for r in range(1, 8):
        pl.semaphore_signal(
            barrier, inc=1, device_id=((me + r) % 8, fs), device_id_type=pl.DeviceIdType.MESH
        )
    for r in range(1, 4):
        pl.semaphore_signal(
            barrier, inc=1, device_id=(me, (fs + r) % 4), device_id_type=pl.DeviceIdType.MESH
        )
    pl.semaphore_wait(barrier, 10)

    def remote(src, dst, send, recv, seq, fsdp):
        return pltpu.make_async_remote_copy(
            src_ref=src, dst_ref=dst, send_sem=send, recv_sem=recv,
            device_id=(seq, fsdp), device_id_type=pl.DeviceIdType.MESH,
        )

    def x_cols(f):
        return pl.ds(pl.multiple_of(f * feats, 128), feats)

    def slot(r, f):
        return xg_ref.at[r, :, x_cols(f)]

    def to_temporal(j):
        target = half + j
        r = (me + 8 - target) % 8
        return remote(x_ref.at[j], slot(r, fs), x_send.at[j], x_recv.at[r], target, fs)

    def to_spatial(j):
        target = (me + half) % 8
        return remote(
            x_ref.at[j], slot(half + j, fs), x_send.at[half + j], x_recv.at[half + j], target, fs
        )

    def keep_spatial(j):
        return pltpu.make_async_copy(x_ref.at[j], slot(j, fs), local_sem.at[kinds + j])

    def keep_temporal():
        return pltpu.make_async_copy(x_ref.at[me % half], slot(0, fs), local_sem.at[kinds])

    for j in range(half):
        @pl.when(me != half + j)
        def _():
            to_temporal(j).start()

        @pl.when(is_temporal)
        def _():
            to_spatial(j).start()

        @pl.when(is_spatial)
        def _():
            keep_spatial(j).start()

    @pl.when(is_temporal)
    def _():
        keep_temporal().start()

    def mate_copy(i):
        return remote(own_ref.at[i], wg_ref.at[i, me], mate_send.at[i], mate_recv.at[i], mate, fs)

    def relay_copy(i):
        return remote(oth_ref.at[i], relay_ref.at[i], cross_send.at[i], relay_recv.at[i], mate, fs)

    def cross_copy(i):
        return remote(oth_ref.at[i], wg_ref.at[i, me], cross_send.at[i], a1_recv.at[i], a1, fs)

    def fwd_copy(i):
        return remote(relay_ref.at[i], wg_ref.at[i, mate], fwd_send.at[i], a2_recv.at[i], a1, fs)

    def a1_copy(i):
        at = wg_ref.at[i, a1]
        return remote(at, at, a1_send.at[i], a1_recv.at[i], mate, fs)

    def a2_copy(i):
        at = wg_ref.at[i, a2]
        return remote(at, at, a2_send.at[i], a2_recv.at[i], mate, fs)

    def y_copy(i, k):
        row = (me, mate, a1, a2)[k]
        src = own_ref.at[i] if k == 0 else wg_ref.at[i, row]
        return remote(src, wg_ref.at[i, row], y_send.at[i, k], y_recv.at[i, k], other_y, fs)

    def keep_w(i):
        return pltpu.make_async_copy(own_ref.at[i], wg_ref.at[i, me], local_sem.at[i])

    def start_w(i):
        mate_copy(i).start()

        @pl.when(outer)
        def _():
            relay_copy(i).start()

        @pl.when(inner)
        def _():
            cross_copy(i).start()

        y_copy(i, 0).start()
        keep_w(i).start()

    def forward_w(i):
        mate_copy(i).wait_recv()
        y_copy(i, 1).start()

        @pl.when(inner)
        def _():
            relay_copy(i).wait_recv()
            fwd_copy(i).start()

        a1_copy(i).wait_recv()

        @pl.when(inner)
        def _():
            a1_copy(i).start()

        y_copy(i, 2).start()

    def forward_last(i):
        a2_copy(i).wait_recv()

        @pl.when(inner)
        def _():
            a2_copy(i).start()

        y_copy(i, 3).start()

    start_w(0)
    start_w(1)

    def near_copy(r):
        return remote(slot(r, fs), slot(r, fs), near_send.at[r], near_recv.at[r], me, across)

    def core_copy(r):
        return remote(slot(r, fs), slot(r, fs), core_send.at[r], core_recv.at[r], me, sib)

    def pass_copy(r):
        at = slot(r, across)
        return remote(at, at, pass_send.at[r], pass_recv.at[r], me, sib)

    def x_arrived(r):
        remote(x_ref.at[0], slot(r, fs), x_send.at[0], x_recv.at[r], me, across).wait_recv()

    for r in range(8):
        if r == 0:
            @pl.when(is_temporal)
            def _():
                keep_temporal().wait()
        else:
            @pl.when(is_temporal)
            def _():
                x_arrived(r)
        if r < half:
            @pl.when(is_spatial)
            def _():
                keep_spatial(r).wait()
        else:
            @pl.when(is_spatial)
            def _():
                x_arrived(r)
        near_copy(r).start()
        core_copy(r).start()

    forward_w(0)
    forward_w(1)
    start_w(2)

    for r in range(8):
        remote(
            slot(r, across), slot(r, across), near_send.at[r], near_recv.at[r], me, across
        ).wait_recv()
        pass_copy(r).start()

    forward_last(0)
    forward_last(1)

    for r in range(8):
        core_copy(r).wait_recv()
        pass_copy(r).wait_recv()

    def multiply(i, k):
        if k == 0:
            keep_w(i).wait()
        y_copy(i, k).wait_recv()
        at_z = ((me, mate, a1, a2)[k]) // 2
        cols = pl.ds(pl.multiple_of(at_z * feats, 128), feats)

        def rows(t, carry):
            at = pl.ds(t * half, half)
            left = xg_ref[at, :, cols].reshape(half * quarter, feats)
            right = wg_ref[i, pl.ds(at_z * 2, 2)].reshape(feats, wg_ref.shape[3])
            term = jnp.dot(left, right, preferred_element_type=jnp.float32)
            term = term.reshape(half, quarter, wg_ref.shape[3])
            if k == 0:
                total[i, at] = term
            else:
                total[i, at] = total[i, at] + term
            return carry

        lax.fori_loop(0, 2, rows, 0)

    for k in range(3):
        multiply(0, k)
        multiply(1, k)
    forward_w(2)
    multiply(0, 3)
    multiply(1, 3)

    ones = jnp.ones((8, wg_ref.shape[3]), jnp.bfloat16)
    last = (((1,), (1,)), ((), ()))

    def sum_slot(r, carry):
        for i in range(2):
            raw = total[i, r]
            square = raw * raw
            high = square.astype(jnp.bfloat16)
            low = (square - high.astype(jnp.float32)).astype(jnp.bfloat16)
            found = lax.dot_general(ones, high, last, preferred_element_type=jnp.float32)
            found = found + lax.dot_general(ones, low, last, preferred_element_type=jnp.float32)
            sq[r, i] = jnp.concatenate(
                [found, jnp.zeros((8, sq.shape[3] - quarter), jnp.float32)], axis=1
            )
        return carry

    lax.fori_loop(0, 8, sum_slot, 0)

    def cast_copy(p):
        return remote(sq, sq_in.at[p], cast_send.at[p], cast_recv.at[p], me, (fs + p + 1) % 4)

    for p in range(3):
        cast_copy(p).start()
    forward_last(2)
    for k in range(2):
        multiply(2, k)
    for p in range(3):
        cast_copy(p).wait_recv()
    sq_out[...] = (sq[...] + sq_in[0]) + (sq_in[1] + sq_in[2])

    def sum_copy(r):
        frame_sp = me + r // half * half
        part = r % half
        to_t = half + part
        at_t = (frame_sp + 2 * 8 - to_t) % 8
        frame_tm = (me + r) % 8
        to_s = frame_tm % half
        at_s = frame_tm // half * half + me % half
        target = jnp.where(is_spatial, to_t, to_s)
        at = jnp.where(is_spatial, at_t, at_s)
        return remote(sq_out.at[r], sq_in.at[3, at], sum_send.at[r], sum_recv.at[at], target, fs)

    def sum_came(r):
        return remote(sq_out.at[r], sq_in.at[3, r], sum_send.at[r], sum_recv.at[r], (me + 1) % 8, fs)

    for r in range(8):
        sum_copy(r).start()
    for k in range(2, 4):
        multiply(2, k)
    for r in range(8):
        sum_came(r).wait_recv()

    def norm_slot(r, carry):
        for i, out in ((0, q_ref), (1, k_ref)):
            whole = sq_out[r, i] + sq_in[3, r, i]
            scale = lax.rsqrt(whole / (H * HD) + 1e-06)
            scale = jnp.transpose(scale)[:quarter, :1]
            out[r] = (total[i, r] * scale * gain_ref[i]).astype(jnp.bfloat16)
        v_ref[r] = total[2, r].astype(jnp.bfloat16)
        return carry

    lax.fori_loop(0, 8, norm_slot, 0)

    for r in range(8):
        sum_copy(r).wait_send()
        near_copy(r).wait_send()
        core_copy(r).wait_send()
        pass_copy(r).wait_send()
    for p in range(3):
        cast_copy(p).wait_send()
    for j in range(half):
        @pl.when(me != half + j)
        def _():
            to_temporal(j).wait_send()

        @pl.when(is_temporal)
        def _():
            to_spatial(j).wait_send()

    for i in range(kinds):
        mate_copy(i).wait_send()
        cross_copy(i).wait_send()

        @pl.when(inner)
        def _():
            fwd_copy(i).wait_send()
            a1_copy(i).wait_send()
            a2_copy(i).wait_send()

        for k in range(4):
            y_copy(i, k).wait_send()


def project(x_quarters, w_own, w_oth, gains, seq_count, fsdp_count):
    half, quarter, feats = x_quarters.shape
    kinds, rows, cols = w_own.shape
    dma = pltpu.SemaphoreType.DMA
    any_spec = pl.BlockSpec(memory_space=pl.ANY)
    near = pl.BlockSpec(memory_space=pltpu.VMEM)
    sent = jnp.bfloat16
    lanes = -(-quarter // 128) * 128
    sums = (seq_count, 2, 8, lanes)
    return pl.pallas_call(
        project_kernel,
        out_shape=[jax.ShapeDtypeStruct((seq_count, quarter, cols), sent)] * 3,
        in_specs=[any_spec] * 3 + [near],
        out_specs=[near] * 3,
        scratch_shapes=[
            pltpu.VMEM((seq_count, quarter, feats * fsdp_count), sent),
            pltpu.VMEM((kinds, seq_count, rows, cols), sent),
            pltpu.VMEM((kinds, rows, cols), sent),
            pltpu.VMEM((kinds, seq_count, quarter, cols), jnp.float32),
            pltpu.VMEM(sums, jnp.float32),
            pltpu.VMEM((4,) + sums, jnp.float32),
            pltpu.VMEM(sums, jnp.float32),
        ]
        + [dma((8,))] * 8
        + [dma((3,))] * 2
        + [dma((kinds,))] * 9
        + [dma((kinds, 4)), dma((kinds, 4)), dma((8,)), dma((8,)), dma((kinds + half,))],
        compiler_params=pltpu.CompilerParams(
            collective_id=0, has_side_effects=True, vmem_limit_bytes=60 * 1024 * 1024
        ),
    )(x_quarters, w_own, w_oth, gains)


def pick_heads(array, heads):
    return jnp.concatenate(
        [lax.dynamic_slice_in_dim(array, head * HD, HD, axis=array.ndim - 1) for head in heads],
        axis=-1,
    )


def split_shards(x_tokens, w_qkv, q_gain, k_gain, head_kind, block_live):
    seq_count = lax.axis_size("seq")
    half = seq_count // 2
    me = lax.axis_index("seq")
    z, y = me // 2, me % 2
    is_spatial = me < half
    rows, feats = x_tokens.shape
    quarter = rows // half
    head_count = head_kind.shape[0]
    kept = head_count // 2
    all_heads = jnp.arange(head_count)
    kinds = (head_kind > 0).astype(jnp.int32)
    before = all_heads[None, :] < all_heads[:, None]
    tm_before = jnp.sum(jnp.where(before, kinds[None, :], 0), axis=1)
    place = jnp.where(kinds > 0, kept + tm_before, all_heads - tm_before)
    order = jnp.sum(
        jnp.where(place[None, :] == all_heads[:, None], all_heads[None, :], 0), axis=1
    )
    sp_heads = [order[i] for i in range(kept)]
    tm_heads = [order[kept + i] for i in range(kept)]
    my_heads = [jnp.where(is_spatial, s, t) for s, t in zip(sp_heads, tm_heads)]

    other_heads = [jnp.where(is_spatial, t, s) for s, t in zip(sp_heads, tm_heads)]

    gains = jnp.stack([pick_heads(q_gain, my_heads), pick_heads(k_gain, my_heads)])
    queries, keys_n, values = project(
        x_tokens.reshape(half, quarter, feats),
        pick_heads(w_qkv, my_heads),
        pick_heads(w_qkv, other_heads),
        gains[:, None, :],
        seq_count,
        lax.axis_size("fsdp"),
    )

    up_half = [(i + half, i) for i in range(half)]
    live = block_live[0]
    live_two = jnp.stack([live, lax.ppermute(live, "seq", up_half)])
    live_two = jnp.take(live_two, order[:kept], axis=1)
    bias = jnp.where(live_two.reshape(2, kept, -1) > 0, 0.0, -1e30).astype(jnp.float32)
    role = is_spatial.astype(jnp.int32).reshape(1)
    done = attend(role, bias, queries, keys_n, values)

    back = lax.ppermute(done[half:], "seq", [(i, i + half) for i in range(half)])
    spatial = jnp.where(is_spatial, done[:half], back).reshape(rows, kept * HD)
    came = [done[:1]]
    for r in range(1, seq_count):
        came.append(
            lax.ppermute(
                done[r : r + 1], "seq", [(s, (s + r) % seq_count) for s in range(half, seq_count)]
            )
        )
    came = jnp.concatenate(came, axis=0)
    came_at = (me - half - jnp.arange(half)) % seq_count
    temporal = jnp.take(came, came_at, axis=0).reshape(rows, kept * HD)
    both = jnp.concatenate([spatial, temporal], axis=1)
    return pick_heads(both, [place[h] for h in range(head_count)])


def solution(mesh):
    placed = (
        P("seq", "fsdp"),
        P(None, "seq", "fsdp"),
        P("fsdp"),
        P("fsdp"),
        P("fsdp"),
        P("seq", "fsdp", None, None),
    )

    def chosen(x_tokens, w_qkv, q_gain, k_gain, head_kind, block_live):
        fits = (
            mesh.shape["seq"] == 8
            and head_kind.shape[0] == 10
            and block_live.shape[0] == 1
            and x_tokens.shape[1] * mesh.shape["fsdp"] == w_qkv.shape[1] * mesh.shape["seq"]
            and mesh.shape["fsdp"] == 4
        )
        body = split_shards if fits else shards
        return body(x_tokens, w_qkv, q_gain, k_gain, head_kind, block_live)

    return jax.shard_map(
        chosen, mesh=mesh, in_specs=placed, out_specs=P("seq", "fsdp"), check_vma=False
    )
```

```python
import math

import jax
import jax.numpy as jnp
from jax import lax
from jax.experimental import pallas as pl
from jax.experimental.pallas import tpu as pltpu
from jax.sharding import PartitionSpec as P

H = 40
HD = 128
BLK = 128


def softmax_rows(scores):
    row_max = jnp.max(scores, axis=-1, keepdims=True)
    expo = jnp.exp(scores - row_max)
    return (expo / jnp.sum(expo, axis=-1, keepdims=True)).astype(jnp.bfloat16)


def spatial_attend(queries, keys_n, values, live_blocks):
    score_scale = 1.0 / math.sqrt(HD)
    scores = (
        jnp.einsum("fqhd,fkhd->fhqk", queries, keys_n, preferred_element_type=jnp.float32)
        * score_scale
    )
    key_mask = jnp.repeat(jnp.repeat(live_blocks, BLK, axis=2), BLK, axis=3)
    scores = jnp.where(key_mask, scores, -1e30)
    sp_weights = softmax_rows(scores)
    return jnp.einsum(
        "fhqk,fkhd->fqhd", sp_weights, values, preferred_element_type=jnp.float32
    ).astype(jnp.bfloat16)


def temporal_attend(triple):
    queries, keys_n, values = triple
    frame_count, single, pos_count, col_width = queries.shape
    head_count = col_width // HD
    grid_shape = (frame_count, pos_count, head_count, HD)
    score_scale = 1.0 / math.sqrt(HD)
    scores = (
        jnp.einsum(
            "fphd,gphd->phfg",
            queries.reshape(grid_shape),
            keys_n.reshape(grid_shape),
            preferred_element_type=jnp.float32,
        )
        * score_scale
    )
    tm_weights = softmax_rows(scores)
    result = jnp.einsum(
        "phfg,gphd->fphd",
        tm_weights,
        values.reshape(grid_shape),
        preferred_element_type=jnp.float32,
    )
    return result.astype(jnp.bfloat16).reshape(frame_count, single, pos_count, col_width)


def shards(x_tokens, w_qkv, q_gain, k_gain, head_kind, block_live):
    full_tokens = lax.all_gather(x_tokens, "fsdp", axis=1, tiled=True)
    tok_rows = full_tokens.shape[0]
    col_width = w_qkv.shape[2]

    def add_rows(shard_rows):
        return jnp.dot(full_tokens, shard_rows, preferred_element_type=jnp.float32)

    q_raw = add_rows(lax.all_gather(w_qkv[0], "seq", axis=0, tiled=True))
    k_raw = add_rows(lax.all_gather(w_qkv[1], "seq", axis=0, tiled=True))
    v_raw = add_rows(lax.all_gather(w_qkv[2], "seq", axis=0, tiled=True))
    q_sq, k_sq = lax.psum((jnp.sum(q_raw * q_raw, axis=1), jnp.sum(k_raw * k_raw, axis=1)), "fsdp")
    total_cols = H * HD
    queries = (q_raw * lax.rsqrt(q_sq[:, None] / total_cols + 1e-06) * q_gain).astype(jnp.bfloat16)
    keys_n = (k_raw * lax.rsqrt(k_sq[:, None] / total_cols + 1e-06) * k_gain).astype(jnp.bfloat16)
    values = v_raw.astype(jnp.bfloat16)
    seq_count = lax.axis_size("seq")
    frames_dev = block_live.shape[0]
    positions = tok_rows // frames_dev
    per_device = positions // seq_count
    head_count = col_width // HD
    live_blocks = block_live > 0

    def to_blocks(columns):
        return columns.reshape(frames_dev, seq_count, per_device, col_width)

    relayed = temporal_attend(
        (
            lax.all_to_all(to_blocks(queries), "seq", split_axis=1, concat_axis=0, tiled=True),
            lax.all_to_all(to_blocks(keys_n), "seq", split_axis=1, concat_axis=0, tiled=True),
            lax.all_to_all(to_blocks(values), "seq", split_axis=1, concat_axis=0, tiled=True),
        )
    )
    returned = lax.all_to_all(relayed, "seq", split_axis=0, concat_axis=1, tiled=True).reshape(
        tok_rows, col_width
    )
    grid_shape = (frames_dev, positions, head_count, HD)
    spatial = spatial_attend(
        queries.reshape(grid_shape),
        keys_n.reshape(grid_shape),
        values.reshape(grid_shape),
        live_blocks,
    )
    is_temporal = jnp.repeat(head_kind > 0, HD)[None, :]
    return jnp.where(is_temporal, returned, spatial.reshape(tok_rows, col_width))

def block_kernel(
    mask_ref, x_ref, w_ref, gain_ref, bias_ref, out_ref,
    xg_ref, wg_ref, oth_ref, relay_ref, total, sq, sq_in, sq_out, bias_in, back,
    x_send, x_recv, near_send, near_recv, core_send, core_recv, pass_send, pass_recv,
    cast_send, cast_recv, mate_send, mate_recv, cross_send, relay_recv, fwd_send, a1_send, a1_recv,
    a2_send, a2_recv, y_send, y_recv, sum_send, sum_recv, local_sem, bias_send, bias_recv,
    back_send, back_recv,
):
    me, fs = lax.axis_index("seq"), lax.axis_index("fsdp")
    quarter, feats = x_ref.shape[1:]
    kinds, _, width = oth_ref.shape
    kept = width // HD
    half = 4
    z, y = me // 2, me % 2
    mate = (z + 1 - 2 * (z % 2)) * 2 + y
    side = z // 2
    a1 = (2 - side) * 2 + y
    a2 = (3 - 3 * side) * 2 + y
    other_y = z * 2 + 1 - y
    inner = (z == 1) | (z == 2)
    outer = (z == 0) | (z == 3)
    is_spatial = me < half
    is_temporal = me >= half
    sib = fs + 1 - 2 * (fs % 2)
    across = (fs + 2) % 4

    barrier = pltpu.get_barrier_semaphore()
    for r in range(1, 8):
        pl.semaphore_signal(
            barrier, inc=1, device_id=((me + r) % 8, fs), device_id_type=pl.DeviceIdType.MESH
        )
    for r in range(1, 4):
        pl.semaphore_signal(
            barrier, inc=1, device_id=(me, (fs + r) % 4), device_id_type=pl.DeviceIdType.MESH
        )
    pl.semaphore_wait(barrier, 10)

    def remote(src, dst, send, recv, seq, fsdp):
        return pltpu.make_async_remote_copy(
            src_ref=src, dst_ref=dst, send_sem=send, recv_sem=recv,
            device_id=(seq, fsdp), device_id_type=pl.DeviceIdType.MESH,
        )

    def x_cols(f):
        return pl.ds(pl.multiple_of(f * feats, 128), feats)

    def slot(r, f):
        return xg_ref.at[r, :, x_cols(f)]

    def to_temporal(j):
        target = half + j
        r = (me + 8 - target) % 8
        return remote(x_ref.at[j], slot(r, fs), x_send.at[j], x_recv.at[r], target, fs)

    def to_spatial(j):
        target = (me + half) % 8
        return remote(
            x_ref.at[j], slot(half + j, fs), x_send.at[half + j], x_recv.at[half + j], target, fs
        )

    def keep_spatial(j):
        return pltpu.make_async_copy(x_ref.at[j], slot(j, fs), local_sem.at[j])

    def keep_temporal():
        return pltpu.make_async_copy(x_ref.at[me % half], slot(0, fs), local_sem.at[0])

    for j in range(half):
        @pl.when(me != half + j)
        def _():
            to_temporal(j).start()

        @pl.when(is_temporal)
        def _():
            to_spatial(j).start()

        @pl.when(is_spatial)
        def _():
            keep_spatial(j).start()

    @pl.when(is_temporal)
    def _():
        keep_temporal().start()

    def mate_copy(i):
        return remote(wg_ref.at[i, me], wg_ref.at[i, me], mate_send.at[i], mate_recv.at[i], mate, fs)

    def relay_copy(i):
        return remote(oth_ref.at[i], relay_ref.at[i], cross_send.at[i], relay_recv.at[i], mate, fs)

    def cross_copy(i):
        return remote(oth_ref.at[i], wg_ref.at[i, me], cross_send.at[i], a1_recv.at[i], a1, fs)

    def fwd_copy(i):
        return remote(relay_ref.at[i], wg_ref.at[i, mate], fwd_send.at[i], a2_recv.at[i], a1, fs)

    def a1_copy(i):
        at = wg_ref.at[i, a1]
        return remote(at, at, a1_send.at[i], a1_recv.at[i], mate, fs)

    def a2_copy(i):
        at = wg_ref.at[i, a2]
        return remote(at, at, a2_send.at[i], a2_recv.at[i], mate, fs)

    def y_copy(i, k):
        row = (me, mate, a1, a2)[k]
        at = wg_ref.at[i, row]
        return remote(at, at, y_send.at[i, k], y_recv.at[i, k], other_y, fs)

    heads = 2 * kept

    def chosen_sum(first, blocks):
        found = None
        for h, block in blocks:
            rows = block.shape[0] // mask_ref.shape[1]
            term = block.reshape(rows, *mask_ref.shape[1:]) * mask_ref[first + h][None]
            found = term if found is None else found + term
        return found.reshape(-1, HD)

    def pick_w(i):
        def cut(h):
            return w_ref[i, :, pl.ds(h * HD, HD)]

        for n in range(kept):
            near_heads = range(n, n + kept + 1)
            to = pl.ds(n * HD, HD)
            wg_ref[i, me, :, to] = chosen_sum(n * heads, [(h, cut(h)) for h in near_heads])
            oth_ref[i, :, to] = chosen_sum((kept + n) * heads, [(h, cut(h)) for h in near_heads])

    def start_w(i):
        mate_copy(i).start()

        @pl.when(outer)
        def _():
            relay_copy(i).start()

        @pl.when(inner)
        def _():
            cross_copy(i).start()

        y_copy(i, 0).start()

    def forward_w(i):
        mate_copy(i).wait_recv()
        y_copy(i, 1).start()

        @pl.when(inner)
        def _():
            relay_copy(i).wait_recv()
            fwd_copy(i).start()

        a1_copy(i).wait_recv()

        @pl.when(inner)
        def _():
            a1_copy(i).start()

        y_copy(i, 2).start()

    def forward_last(i):
        a2_copy(i).wait_recv()

        @pl.when(inner)
        def _():
            a2_copy(i).start()

        y_copy(i, 3).start()

    pick_w(0)
    start_w(0)
    pick_w(1)
    start_w(1)
    pick_w(2)

    def bias_copy():
        return remote(bias_ref, bias_in, bias_send, bias_recv, (me + half) % 8, fs)

    @pl.when(is_temporal)
    def _():
        bias_copy().start()

    def near_copy(r):
        return remote(slot(r, fs), slot(r, fs), near_send.at[r], near_recv.at[r], me, across)

    def core_copy(r):
        return remote(slot(r, fs), slot(r, fs), core_send.at[r], core_recv.at[r], me, sib)

    def pass_copy(r):
        at = slot(r, across)
        return remote(at, at, pass_send.at[r], pass_recv.at[r], me, sib)

    def x_arrived(r):
        remote(x_ref.at[0], slot(r, fs), x_send.at[0], x_recv.at[r], me, across).wait_recv()

    for r in range(8):
        if r == 0:
            @pl.when(is_temporal)
            def _():
                keep_temporal().wait()
        else:
            @pl.when(is_temporal)
            def _():
                x_arrived(r)
        if r < half:
            @pl.when(is_spatial)
            def _():
                keep_spatial(r).wait()
        else:
            @pl.when(is_spatial)
            def _():
                x_arrived(r)
        near_copy(r).start()
        core_copy(r).start()

    forward_w(0)
    forward_w(1)
    start_w(2)

    for r in range(8):
        remote(
            slot(r, across), slot(r, across), near_send.at[r], near_recv.at[r], me, across
        ).wait_recv()
        pass_copy(r).start()

    forward_last(0)
    forward_last(1)

    for r in range(8):
        core_copy(r).wait_recv()
        pass_copy(r).wait_recv()

    def multiply(i, k):
        y_copy(i, k).wait_recv()
        at_z = ((me, mate, a1, a2)[k]) // 2
        cols = pl.ds(pl.multiple_of(at_z * feats, 128), feats)

        def rows(t, carry):
            at = pl.ds(t * half, half)
            left = xg_ref[at, :, cols].reshape(half * quarter, feats)
            right = wg_ref[i, pl.ds(at_z * 2, 2)].reshape(feats, wg_ref.shape[3])
            term = jnp.dot(left, right, preferred_element_type=jnp.float32)
            term = term.reshape(half, quarter, wg_ref.shape[3])
            if k == 0:
                total[i, at] = term
            else:
                total[i, at] = total[i, at] + term
            return carry

        lax.fori_loop(0, 2, rows, 0)

    for k in range(3):
        multiply(0, k)
        multiply(1, k)
    forward_w(2)
    multiply(0, 3)
    multiply(1, 3)

    ones = jnp.ones((8, wg_ref.shape[3]), jnp.bfloat16)
    last = (((1,), (1,)), ((), ()))

    def sum_slot(r, carry):
        for i in range(2):
            raw = total[i, r]
            square = raw * raw
            high = square.astype(jnp.bfloat16)
            low = (square - high.astype(jnp.float32)).astype(jnp.bfloat16)
            found = lax.dot_general(ones, high, last, preferred_element_type=jnp.float32)
            found = found + lax.dot_general(ones, low, last, preferred_element_type=jnp.float32)
            sq[r, i] = jnp.concatenate(
                [found, jnp.zeros((8, sq.shape[3] - quarter), jnp.float32)], axis=1
            )
        return carry

    lax.fori_loop(0, 8, sum_slot, 0)

    def cast_copy(p):
        return remote(sq, sq_in.at[p], cast_send.at[p], cast_recv.at[p], me, (fs + p + 1) % 4)

    for p in range(3):
        cast_copy(p).start()
    forward_last(2)
    for k in range(2):
        multiply(2, k)
    for p in range(3):
        cast_copy(p).wait_recv()
    sq_out[...] = (sq[...] + sq_in[0]) + (sq_in[1] + sq_in[2])

    def sum_copy(r):
        frame_sp = me + r // half * half
        part = r % half
        to_t = half + part
        at_t = (frame_sp + 2 * 8 - to_t) % 8
        frame_tm = (me + r) % 8
        to_s = frame_tm % half
        at_s = frame_tm // half * half + me % half
        target = jnp.where(is_spatial, to_t, to_s)
        at = jnp.where(is_spatial, at_t, at_s)
        return remote(sq_out.at[r], sq_in.at[3, at], sum_send.at[r], sum_recv.at[at], target, fs)

    def sum_came(r):
        return remote(sq_out.at[r], sq_in.at[3, r], sum_send.at[r], sum_recv.at[r], (me + 1) % 8, fs)

    for r in range(8):
        sum_copy(r).start()
    for k in range(2, 4):
        multiply(2, k)
    for r in range(8):
        sum_came(r).wait_recv()

    for r in range(8):
        near_copy(r).wait_send()
        core_copy(r).wait_send()
        pass_copy(r).wait_send()

    def norm_slot(r, carry):
        for i in range(2):
            whole = sq_out[r, i] + sq_in[3, r, i]
            scale = lax.rsqrt(whole / (H * HD) + 1e-06)
            scale = jnp.transpose(scale)[:quarter, :1]
            normed = (total[i, r] * scale * gain_ref[i]).astype(jnp.bfloat16)
            xg_ref[r, :, pl.ds(i * width, width)] = normed
        xg_ref[r, :, pl.ds(2 * width, width)] = total[2, r].astype(jnp.bfloat16)
        return carry

    lax.fori_loop(0, 8, norm_slot, 0)

    factor = math.log2(math.e) / math.sqrt(HD)

    def head_cols(i, h):
        return pl.ds(pl.multiple_of(i * width + h * HD, HD), HD)

    def weigh(scores, vals):
        row_max = jnp.max(scores, axis=-1, keepdims=True)
        expo = jnp.exp2(scores - row_max)
        inverse = 1.0 / jnp.sum(expo, axis=-1, keepdims=True)
        mixed = jnp.dot(expo.astype(jnp.bfloat16), vals, preferred_element_type=jnp.float32)
        return (mixed * inverse).astype(jnp.bfloat16)

    frame_rows = half * quarter

    def spatial_frame(frame, mask_ref):
        at = pl.ds(frame * half, half)

        def one_head(h, carry):
            qs, ks, vs = [
                xg_ref[at, :, head_cols(i, h)].reshape(frame_rows, HD) for i in range(3)
            ]
            pieces = []
            for qb in range(frame_rows // BLK):
                scores = lax.dot_general(
                    qs[qb * BLK : (qb + 1) * BLK], ks, last, preferred_element_type=jnp.float32
                )
                pieces.append(weigh(scores * factor + mask_ref[h, pl.ds(qb, 1)], vs))
            res = jnp.concatenate(pieces, axis=0).reshape(half, quarter, HD)
            if frame == 0:
                back[:, :, head_cols(0, h)] = res
            else:
                xg_ref[at, :, head_cols(3, h)] = res
            return carry

        lax.fori_loop(0, kept, one_head, 0)

    step = 32
    mix = 8 * step

    def temporal_all():
        row_pos = lax.broadcasted_iota(jnp.int32, (mix, mix), 0) % step
        col_pos = lax.broadcasted_iota(jnp.int32, (mix, mix), 1) % step
        hide = jnp.where(row_pos == col_pos, 0.0, -1e30)

        def one_head(h, carry):
            for pb in range(quarter // step):
                at = pl.ds(pb * step, step)
                qs, ks, vs = [
                    xg_ref[:, at, head_cols(i, h)].reshape(mix, HD) for i in range(3)
                ]
                scores = lax.dot_general(qs, ks, last, preferred_element_type=jnp.float32)
                res = weigh(scores * factor + hide, vs)
                xg_ref[:, at, head_cols(3, h)] = res.reshape(8, step, HD)
            return carry

        lax.fori_loop(0, kept, one_head, 0)

    def back_spatial():
        return remote(
            xg_ref.at[pl.ds(half, half), :, pl.ds(3 * width, width)],
            back.at[:, :, pl.ds(0, width)],
            back_send.at[0], back_recv.at[0], (me + half) % 8, fs,
        )

    def back_temporal(r):
        return remote(
            xg_ref.at[r, :, pl.ds(3 * width, width)],
            back.at[me % half, :, pl.ds(width, width)],
            back_send.at[r], back_recv.at[1 + me % half], (me + r) % 8, fs,
        )

    def back_came(q):
        return remote(
            xg_ref.at[0, :, pl.ds(3 * width, width)],
            back.at[q, :, pl.ds(width, width)],
            back_send.at[0], back_recv.at[1 + q], (me + 1) % 8, fs,
        )

    @pl.when(is_spatial)
    def _():
        bias_copy().wait_recv()
        spatial_frame(1, bias_in)
        back_spatial().start()
        spatial_frame(0, bias_ref)

    @pl.when(is_temporal)
    def _():
        temporal_all()
        for r in range(1, 8):
            back_temporal(r).start()
        back[me % half, :, pl.ds(width, width)] = xg_ref[0, :, pl.ds(3 * width, width)]
        bias_copy().wait_send()
        back_spatial().wait_recv()

    for q in range(half):
        @pl.when(me != half + q)
        def _():
            back_came(q).wait_recv()

    for h in range(heads):
        ranks = [n for n in range(kept) if n <= h <= n + kept]
        blocks = [
            (p, back[:, :, pl.ds(p * HD, HD)].reshape(frame_rows, HD))
            for p in ranks + [kept + n for n in ranks]
        ]
        res = chosen_sum((heads + h) * heads, blocks)
        out_ref[:, :, pl.ds(h * HD, HD)] = res.reshape(half, quarter, HD)

    @pl.when(is_spatial)
    def _():
        back_spatial().wait_send()

    @pl.when(is_temporal)
    def _():
        for r in range(1, 8):
            back_temporal(r).wait_send()

    for r in range(8):
        sum_copy(r).wait_send()
    for p in range(3):
        cast_copy(p).wait_send()
    for j in range(half):
        @pl.when(me != half + j)
        def _():
            to_temporal(j).wait_send()

        @pl.when(is_temporal)
        def _():
            to_spatial(j).wait_send()

    for i in range(kinds):
        mate_copy(i).wait_send()
        cross_copy(i).wait_send()

        @pl.when(inner)
        def _():
            fwd_copy(i).wait_send()
            a1_copy(i).wait_send()
            a2_copy(i).wait_send()

        for k in range(4):
            y_copy(i, k).wait_send()


def attend_block(masks, x_quarters, w_qkv, gains, bias, seq_count, fsdp_count):
    half, quarter, feats = x_quarters.shape
    kinds, rows, _ = w_qkv.shape
    cols = gains.shape[-1]
    dma = pltpu.SemaphoreType.DMA
    near = pl.BlockSpec(memory_space=pltpu.VMEM)
    sent = jnp.bfloat16
    lanes = -(-quarter // 128) * 128
    sums = (seq_count, 2, 8, lanes)
    return pl.pallas_call(
        block_kernel,
        out_shape=jax.ShapeDtypeStruct((half, quarter, 2 * cols), sent),
        in_specs=[
            near,
            pl.BlockSpec(memory_space=pl.ANY),
            near,
            near,
            near,
        ],
        out_specs=near,
        scratch_shapes=[
            pltpu.VMEM((seq_count, quarter, feats * fsdp_count), sent),
            pltpu.VMEM((kinds, seq_count, rows, cols), sent),
            pltpu.VMEM((kinds, rows, cols), sent),
            pltpu.VMEM((kinds, rows, cols), sent),
            pltpu.VMEM((kinds, seq_count, quarter, cols), jnp.float32),
            pltpu.VMEM(sums, jnp.float32),
            pltpu.VMEM((4,) + sums, jnp.float32),
            pltpu.VMEM(sums, jnp.float32),
            pltpu.VMEM(bias.shape, jnp.float32),
            pltpu.VMEM((half, quarter, 2 * cols), sent),
        ]
        + [dma((8,))] * 8
        + [dma((3,))] * 2
        + [dma((kinds,))] * 9
        + [dma((kinds, 4)), dma((kinds, 4)), dma((8,)), dma((8,)), dma((half,))]
        + [dma, dma, dma((8,)), dma((8,))],
        compiler_params=pltpu.CompilerParams(
            collective_id=0, has_side_effects=True, vmem_limit_bytes=61 * 1024 * 1024
        ),
    )(masks, x_quarters, w_qkv, gains, bias)


def split_shards(x_tokens, w_qkv, q_gain, k_gain, head_kind, block_live):
    seq_count = lax.axis_size("seq")
    half = seq_count // 2
    me = lax.axis_index("seq")
    is_spatial = me < half
    rows, feats = x_tokens.shape
    quarter = rows // half
    head_count = head_kind.shape[0]
    kept = head_count // 2
    all_heads = jnp.arange(head_count)
    kinds = (head_kind > 0).astype(jnp.int32)
    before = all_heads[None, :] < all_heads[:, None]
    tm_before = jnp.sum(jnp.where(before, kinds[None, :], 0), axis=1)
    place = jnp.where(kinds > 0, kept + tm_before, all_heads - tm_before)
    order = jnp.sum(
        jnp.where(place[None, :] == all_heads[:, None], all_heads[None, :], 0), axis=1
    )
    flip = jnp.where(is_spatial, 0, kept)
    slots = jnp.arange(head_count)
    wanted = jnp.where(slots[:, None] == (slots[None, :] + flip) % head_count, order[:, None], 0)
    ordered = jnp.sum(wanted, axis=0)
    mine = ordered[:kept, None] == all_heads[None, :]
    both_gains = jnp.stack([q_gain, k_gain]).reshape(2, 1, head_count, HD)
    gains = jnp.sum(jnp.where(mine[None, :, :, None], both_gains, 0.0), axis=2)
    live = block_live[0].astype(jnp.float32)
    chosen = order[:kept, None] == all_heads[None, :]
    live = jnp.sum(jnp.where(chosen[:, :, None, None], live[None], 0.0), axis=1)
    bias = jnp.repeat(jnp.where(live > 0, 0.0, -1e30), BLK, axis=2)
    bias = jnp.pad(bias, ((0, 0), (0, -bias.shape[1] % 8), (0, 0)))
    at_heads = jnp.concatenate([ordered, place])[:, None] == all_heads[None, :]
    masks = jnp.broadcast_to(
        at_heads.astype(jnp.bfloat16).reshape(-1, 1, 1), (at_heads.size, 16, HD)
    )
    done = attend_block(
        masks,
        x_tokens.reshape(half, quarter, feats),
        w_qkv,
        gains.reshape(2, 1, kept * HD),
        bias,
        seq_count,
        lax.axis_size("fsdp"),
    )
    return done.reshape(rows, head_count * HD)


def solution(mesh):
    placed = (
        P("seq", "fsdp"),
        P(None, "seq", "fsdp"),
        P("fsdp"),
        P("fsdp"),
        P("fsdp"),
        P("seq", "fsdp", None, None),
    )

    def chosen(x_tokens, w_qkv, q_gain, k_gain, head_kind, block_live):
        fits = (
            mesh.shape["seq"] == 8
            and head_kind.shape[0] == 10
            and block_live.shape[0] == 1
            and x_tokens.shape[1] * mesh.shape["fsdp"] == w_qkv.shape[1] * mesh.shape["seq"]
            and mesh.shape["fsdp"] == 4
        )
        body = split_shards if fits else shards
        return body(x_tokens, w_qkv, q_gain, k_gain, head_kind, block_live)

    return jax.shard_map(
        chosen, mesh=mesh, in_specs=placed, out_specs=P("seq", "fsdp"), check_vma=False
    )
```

```python
import math

import jax
import jax.numpy as jnp
from jax import lax
from jax.experimental import pallas as pl
from jax.experimental.pallas import tpu as pltpu
from jax.sharding import PartitionSpec as P

H = 40
HD = 128
BLK = 128


def softmax_rows(scores):
    row_max = jnp.max(scores, axis=-1, keepdims=True)
    expo = jnp.exp(scores - row_max)
    return (expo / jnp.sum(expo, axis=-1, keepdims=True)).astype(jnp.bfloat16)


def spatial_attend(queries, keys_n, values, live_blocks):
    score_scale = 1.0 / math.sqrt(HD)
    scores = (
        jnp.einsum("fqhd,fkhd->fhqk", queries, keys_n, preferred_element_type=jnp.float32)
        * score_scale
    )
    key_mask = jnp.repeat(jnp.repeat(live_blocks, BLK, axis=2), BLK, axis=3)
    scores = jnp.where(key_mask, scores, -1e30)
    sp_weights = softmax_rows(scores)
    return jnp.einsum(
        "fhqk,fkhd->fqhd", sp_weights, values, preferred_element_type=jnp.float32
    ).astype(jnp.bfloat16)


def temporal_attend(triple):
    queries, keys_n, values = triple
    frame_count, single, pos_count, col_width = queries.shape
    head_count = col_width // HD
    grid_shape = (frame_count, pos_count, head_count, HD)
    score_scale = 1.0 / math.sqrt(HD)
    scores = (
        jnp.einsum(
            "fphd,gphd->phfg",
            queries.reshape(grid_shape),
            keys_n.reshape(grid_shape),
            preferred_element_type=jnp.float32,
        )
        * score_scale
    )
    tm_weights = softmax_rows(scores)
    result = jnp.einsum(
        "phfg,gphd->fphd",
        tm_weights,
        values.reshape(grid_shape),
        preferred_element_type=jnp.float32,
    )
    return result.astype(jnp.bfloat16).reshape(frame_count, single, pos_count, col_width)


def shards(x_tokens, w_qkv, q_gain, k_gain, head_kind, block_live):
    full_tokens = lax.all_gather(x_tokens, "fsdp", axis=1, tiled=True)
    tok_rows = full_tokens.shape[0]
    col_width = w_qkv.shape[2]

    def add_rows(shard_rows):
        return jnp.dot(full_tokens, shard_rows, preferred_element_type=jnp.float32)

    q_raw = add_rows(lax.all_gather(w_qkv[0], "seq", axis=0, tiled=True))
    k_raw = add_rows(lax.all_gather(w_qkv[1], "seq", axis=0, tiled=True))
    v_raw = add_rows(lax.all_gather(w_qkv[2], "seq", axis=0, tiled=True))
    q_sq, k_sq = lax.psum((jnp.sum(q_raw * q_raw, axis=1), jnp.sum(k_raw * k_raw, axis=1)), "fsdp")
    total_cols = H * HD
    queries = (q_raw * lax.rsqrt(q_sq[:, None] / total_cols + 1e-06) * q_gain).astype(jnp.bfloat16)
    keys_n = (k_raw * lax.rsqrt(k_sq[:, None] / total_cols + 1e-06) * k_gain).astype(jnp.bfloat16)
    values = v_raw.astype(jnp.bfloat16)
    seq_count = lax.axis_size("seq")
    frames_dev = block_live.shape[0]
    positions = tok_rows // frames_dev
    per_device = positions // seq_count
    head_count = col_width // HD
    live_blocks = block_live > 0

    def to_blocks(columns):
        return columns.reshape(frames_dev, seq_count, per_device, col_width)

    relayed = temporal_attend(
        (
            lax.all_to_all(to_blocks(queries), "seq", split_axis=1, concat_axis=0, tiled=True),
            lax.all_to_all(to_blocks(keys_n), "seq", split_axis=1, concat_axis=0, tiled=True),
            lax.all_to_all(to_blocks(values), "seq", split_axis=1, concat_axis=0, tiled=True),
        )
    )
    returned = lax.all_to_all(relayed, "seq", split_axis=0, concat_axis=1, tiled=True).reshape(
        tok_rows, col_width
    )
    grid_shape = (frames_dev, positions, head_count, HD)
    spatial = spatial_attend(
        queries.reshape(grid_shape),
        keys_n.reshape(grid_shape),
        values.reshape(grid_shape),
        live_blocks,
    )
    is_temporal = jnp.repeat(head_kind > 0, HD)[None, :]
    return jnp.where(is_temporal, returned, spatial.reshape(tok_rows, col_width))

def block_kernel(
    mask_ref, x_ref, w_ref, gain_ref, bias_ref, out_ref,
    xg_ref, wg_ref, oth_ref, relay_ref, total, sq, sq_in, sq_out, bias_in, back,
    x_send, x_recv, near_send, near_recv, core_send, core_recv, pass_send, pass_recv,
    cast_send, cast_recv, mate_send, mate_recv, cross_send, relay_recv, fwd_send, a1_send, a1_recv,
    a2_send, a2_recv, y_send, y_recv, sum_send, sum_recv, local_sem, bias_send, bias_recv,
    back_send, back_recv,
):
    me, fs = lax.axis_index("seq"), lax.axis_index("fsdp")
    quarter, feats = x_ref.shape[1:]
    kinds, _, width = oth_ref.shape
    kept = width // HD
    half = 4
    z, y = me // 2, me % 2
    mate = (z + 1 - 2 * (z % 2)) * 2 + y
    side = z // 2
    a1 = (2 - side) * 2 + y
    a2 = (3 - 3 * side) * 2 + y
    other_y = z * 2 + 1 - y
    inner = (z == 1) | (z == 2)
    outer = (z == 0) | (z == 3)
    is_spatial = me < half
    is_temporal = me >= half
    sib = fs + 1 - 2 * (fs % 2)
    across = (fs + 2) % 4

    barrier = pltpu.get_barrier_semaphore()
    for r in range(1, 8):
        pl.semaphore_signal(
            barrier, inc=1, device_id=((me + r) % 8, fs), device_id_type=pl.DeviceIdType.MESH
        )
    for r in range(1, 4):
        pl.semaphore_signal(
            barrier, inc=1, device_id=(me, (fs + r) % 4), device_id_type=pl.DeviceIdType.MESH
        )
    pl.semaphore_wait(barrier, 10)

    def remote(src, dst, send, recv, seq, fsdp):
        return pltpu.make_async_remote_copy(
            src_ref=src, dst_ref=dst, send_sem=send, recv_sem=recv,
            device_id=(seq, fsdp), device_id_type=pl.DeviceIdType.MESH,
        )

    def x_cols(f):
        return pl.ds(pl.multiple_of(f * feats, 128), feats)

    def slot(r, f):
        return xg_ref.at[r, :, x_cols(f)]

    def to_temporal(j):
        target = half + j
        r = (me + 8 - target) % 8
        return remote(x_ref.at[j], slot(r, fs), x_send.at[j], x_recv.at[r], target, fs)

    def to_spatial(j):
        target = (me + half) % 8
        return remote(
            x_ref.at[j], slot(half + j, fs), x_send.at[half + j], x_recv.at[half + j], target, fs
        )

    def keep_spatial(j):
        return pltpu.make_async_copy(x_ref.at[j], slot(j, fs), local_sem.at[j])

    def keep_temporal():
        return pltpu.make_async_copy(x_ref.at[me % half], slot(0, fs), local_sem.at[0])

    for j in range(half):
        @pl.when(me != half + j)
        def _():
            to_temporal(j).start()

        @pl.when(is_temporal)
        def _():
            to_spatial(j).start()

        @pl.when(is_spatial)
        def _():
            keep_spatial(j).start()

    @pl.when(is_temporal)
    def _():
        keep_temporal().start()

    early = (kept + 1) // 2
    cut_at = early * HD
    parts = ((0, 0, width), (1, 0, width), (2, 0, cut_at), (2, cut_at, width - cut_at))

    def held(c, row):
        i, low, size = parts[c]
        return wg_ref.at[i, row, :, pl.ds(low, size)]

    def loose(ref, c):
        i, low, size = parts[c]
        return ref.at[i, :, pl.ds(low, size)]

    def mate_copy(c):
        return remote(held(c, me), held(c, me), mate_send.at[c], mate_recv.at[c], mate, fs)

    def relay_copy(c):
        return remote(
            loose(oth_ref, c), loose(relay_ref, c), cross_send.at[c], relay_recv.at[c], mate, fs
        )

    def cross_copy(c):
        return remote(loose(oth_ref, c), held(c, me), cross_send.at[c], a1_recv.at[c], a1, fs)

    def fwd_copy(c):
        return remote(loose(relay_ref, c), held(c, mate), fwd_send.at[c], a2_recv.at[c], a1, fs)

    def a1_copy(c):
        return remote(held(c, a1), held(c, a1), a1_send.at[c], a1_recv.at[c], mate, fs)

    def a2_copy(c):
        return remote(held(c, a2), held(c, a2), a2_send.at[c], a2_recv.at[c], mate, fs)

    def y_copy(c, k):
        at = held(c, (me, mate, a1, a2)[k])
        return remote(at, at, y_send.at[c, k], y_recv.at[c, k], other_y, fs)

    heads = 2 * kept

    def chosen_sum(first, blocks):
        found = None
        for h, block in blocks:
            rows = block.shape[0] // mask_ref.shape[1]
            term = block.reshape(rows, *mask_ref.shape[1:]) * mask_ref[first + h][None]
            found = term if found is None else found + term
        return found.reshape(-1, HD)

    def pick_w(i):
        def cut(h):
            return w_ref[i, :, pl.ds(h * HD, HD)]

        for n in range(kept):
            near_heads = range(n, n + kept + 1)
            to = pl.ds(n * HD, HD)
            wg_ref[i, me, :, to] = chosen_sum(n * heads, [(h, cut(h)) for h in near_heads])
            oth_ref[i, :, to] = chosen_sum((kept + n) * heads, [(h, cut(h)) for h in near_heads])

    def start_w(i):
        mate_copy(i).start()

        @pl.when(outer)
        def _():
            relay_copy(i).start()

        @pl.when(inner)
        def _():
            cross_copy(i).start()

        y_copy(i, 0).start()

    def forward_w(i):
        mate_copy(i).wait_recv()
        y_copy(i, 1).start()

        @pl.when(inner)
        def _():
            relay_copy(i).wait_recv()
            fwd_copy(i).start()

        a1_copy(i).wait_recv()

        @pl.when(inner)
        def _():
            a1_copy(i).start()

        y_copy(i, 2).start()

    def forward_last(i):
        a2_copy(i).wait_recv()

        @pl.when(inner)
        def _():
            a2_copy(i).start()

        y_copy(i, 3).start()

    pick_w(0)
    start_w(0)
    pick_w(1)
    start_w(1)
    pick_w(2)

    def bias_copy():
        return remote(bias_ref, bias_in, bias_send, bias_recv, (me + half) % 8, fs)

    @pl.when(is_temporal)
    def _():
        bias_copy().start()

    def near_copy(r):
        return remote(slot(r, fs), slot(r, fs), near_send.at[r], near_recv.at[r], me, across)

    def core_copy(r):
        return remote(slot(r, fs), slot(r, fs), core_send.at[r], core_recv.at[r], me, sib)

    def pass_copy(r):
        at = slot(r, across)
        return remote(at, at, pass_send.at[r], pass_recv.at[r], me, sib)

    def x_arrived(r):
        remote(x_ref.at[0], slot(r, fs), x_send.at[0], x_recv.at[r], me, across).wait_recv()

    for r in range(8):
        if r == 0:
            @pl.when(is_temporal)
            def _():
                keep_temporal().wait()
        else:
            @pl.when(is_temporal)
            def _():
                x_arrived(r)
        if r < half:
            @pl.when(is_spatial)
            def _():
                keep_spatial(r).wait()
        else:
            @pl.when(is_spatial)
            def _():
                x_arrived(r)
        near_copy(r).start()
        core_copy(r).start()

    forward_w(0)
    forward_w(1)
    start_w(2)
    start_w(3)

    for r in range(8):
        remote(
            slot(r, across), slot(r, across), near_send.at[r], near_recv.at[r], me, across
        ).wait_recv()
        pass_copy(r).start()

    forward_last(0)
    forward_last(1)

    for r in range(8):
        core_copy(r).wait_recv()
        pass_copy(r).wait_recv()

    def multiply(c, k):
        i, low, size = parts[c]
        y_copy(c, k).wait_recv()
        at_z = ((me, mate, a1, a2)[k]) // 2
        cols = pl.ds(pl.multiple_of(at_z * feats, 128), feats)
        to = pl.ds(low, size)

        def rows(t, carry):
            at = pl.ds(t * half, half)
            left = xg_ref[at, :, cols].reshape(half * quarter, feats)
            right = wg_ref[i, pl.ds(at_z * 2, 2), :, to].reshape(feats, size)
            term = jnp.dot(left, right, preferred_element_type=jnp.float32)
            term = term.reshape(half, quarter, size)
            if k == 0:
                total[i, at, :, to] = term
            else:
                total[i, at, :, to] = total[i, at, :, to] + term
            return carry

        lax.fori_loop(0, 2, rows, 0)

    def sent_w(c):
        mate_copy(c).wait_send()
        cross_copy(c).wait_send()

        @pl.when(inner)
        def _():
            fwd_copy(c).wait_send()
            a1_copy(c).wait_send()
            a2_copy(c).wait_send()

        for k in range(4):
            y_copy(c, k).wait_send()

    for k in range(3):
        multiply(0, k)
        multiply(1, k)
    forward_w(2)
    multiply(0, 3)
    multiply(1, 3)

    ones = jnp.ones((8, wg_ref.shape[3]), jnp.bfloat16)
    last = (((1,), (1,)), ((), ()))

    def sum_slot(r, carry):
        for i in range(2):
            raw = total[i, r]
            square = raw * raw
            high = square.astype(jnp.bfloat16)
            low = (square - high.astype(jnp.float32)).astype(jnp.bfloat16)
            found = lax.dot_general(ones, high, last, preferred_element_type=jnp.float32)
            found = found + lax.dot_general(ones, low, last, preferred_element_type=jnp.float32)
            sq[r, i] = jnp.concatenate(
                [found, jnp.zeros((8, sq.shape[3] - quarter), jnp.float32)], axis=1
            )
        return carry

    lax.fori_loop(0, 8, sum_slot, 0)

    def cast_copy(p):
        return remote(sq, sq_in.at[p], cast_send.at[p], cast_recv.at[p], me, (fs + p + 1) % 4)

    for p in range(3):
        cast_copy(p).start()
    forward_last(2)
    forward_w(3)
    for k in range(2):
        multiply(2, k)
    for p in range(3):
        cast_copy(p).wait_recv()
    sq_out[...] = (sq[...] + sq_in[0]) + (sq_in[1] + sq_in[2])

    def sum_copy(r):
        frame_sp = me + r // half * half
        part = r % half
        to_t = half + part
        at_t = (frame_sp + 2 * 8 - to_t) % 8
        frame_tm = (me + r) % 8
        to_s = frame_tm % half
        at_s = frame_tm // half * half + me % half
        target = jnp.where(is_spatial, to_t, to_s)
        at = jnp.where(is_spatial, at_t, at_s)
        return remote(sq_out.at[r], sq_in.at[3, at], sum_send.at[r], sum_recv.at[at], target, fs)

    def sum_came(r):
        return remote(sq_out.at[r], sq_in.at[3, r], sum_send.at[r], sum_recv.at[r], (me + 1) % 8, fs)

    for r in range(8):
        sum_copy(r).start()
    for k in range(2, 4):
        multiply(2, k)
    for r in range(8):
        sum_came(r).wait_recv()

    sent_w(0)

    def held_rows(i):
        return pl.ds(i * quarter, quarter)

    def norm_slot(r, carry):
        for i in range(2):
            whole = sq_out[r, i] + sq_in[3, r, i]
            scale = lax.rsqrt(whole / (H * HD) + 1e-06)
            scale = jnp.transpose(scale)[:quarter, :1]
            normed = (total[i, r] * scale * gain_ref[i]).astype(jnp.bfloat16)
            wg_ref[0, r, held_rows(i)] = normed
        return carry

    lax.fori_loop(0, 8, norm_slot, 0)

    def round_values(c):
        _, low, size = parts[c]

        def value_slot(r, carry):
            found = total[2, r, :, pl.ds(low, size)]
            wg_ref[0, r, held_rows(2), pl.ds(low, size)] = found.astype(jnp.bfloat16)
            return carry

        lax.fori_loop(0, 8, value_slot, 0)

    factor = math.log2(math.e) / math.sqrt(HD)

    def head_cols(h):
        return pl.ds(pl.multiple_of(h * HD, HD), HD)

    group_heads = ((0, early), (early, kept))

    def group_cols(g, first=0):
        low, high = group_heads[g]
        return pl.ds(first + low * HD, (high - low) * HD)

    def weigh(scores, vals):
        row_max = jnp.max(scores, axis=-1, keepdims=True)
        expo = jnp.exp2(scores - row_max)
        inverse = 1.0 / jnp.sum(expo, axis=-1, keepdims=True)
        mixed = jnp.dot(expo.astype(jnp.bfloat16), vals, preferred_element_type=jnp.float32)
        return (mixed * inverse).astype(jnp.bfloat16)

    frame_rows = half * quarter

    def spatial_frame(frame, mask_ref, g):
        at = pl.ds(frame * half, half)

        def one_head(h, carry):
            qs, ks, vs = [
                wg_ref[0, at, held_rows(i), head_cols(h)].reshape(frame_rows, HD)
                for i in range(3)
            ]
            pieces = []
            for qb in range(frame_rows // BLK):
                scores = lax.dot_general(
                    qs[qb * BLK : (qb + 1) * BLK], ks, last, preferred_element_type=jnp.float32
                )
                pieces.append(weigh(scores * factor + mask_ref[h, pl.ds(qb, 1)], vs))
            res = jnp.concatenate(pieces, axis=0).reshape(half, quarter, HD)
            if frame == 0:
                back[:, :, head_cols(h)] = res
            else:
                wg_ref[0, at, held_rows(3), head_cols(h)] = res
            return carry

        lax.fori_loop(*group_heads[g], one_head, 0)

    step = 32
    mix = 8 * step

    def temporal_all(g):
        row_pos = lax.broadcasted_iota(jnp.int32, (mix, mix), 0) % step
        col_pos = lax.broadcasted_iota(jnp.int32, (mix, mix), 1) % step
        hide = jnp.where(row_pos == col_pos, 0.0, -1e30)

        def one_head(h, carry):
            for pb in range(quarter // step):
                qs, ks, vs = [
                    wg_ref[0, :, pl.ds(i * quarter + pb * step, step), head_cols(h)].reshape(mix, HD)
                    for i in range(3)
                ]
                scores = lax.dot_general(qs, ks, last, preferred_element_type=jnp.float32)
                res = weigh(scores * factor + hide, vs)
                to = pl.ds(3 * quarter + pb * step, step)
                wg_ref[0, :, to, head_cols(h)] = res.reshape(8, step, HD)
            return carry

        lax.fori_loop(*group_heads[g], one_head, 0)

    def back_spatial(g):
        return remote(
            wg_ref.at[0, pl.ds(half, half), held_rows(3), group_cols(g)],
            back.at[:, :, group_cols(g)],
            back_send.at[g, 0], back_recv.at[g, 0], (me + half) % 8, fs,
        )

    def back_temporal(g, r):
        return remote(
            wg_ref.at[0, r, held_rows(3), group_cols(g)],
            back.at[me % half, :, group_cols(g, width)],
            back_send.at[g, r], back_recv.at[g, 1 + me % half], (me + r) % 8, fs,
        )

    def back_came(g, q):
        return remote(
            wg_ref.at[0, 0, held_rows(3), group_cols(g)],
            back.at[q, :, group_cols(g, width)],
            back_send.at[g, 0], back_recv.at[g, 1 + q], (me + 1) % 8, fs,
        )

    def attend_first(g):
        @pl.when(is_spatial)
        def _():
            if g == 0:
                bias_copy().wait_recv()
            spatial_frame(1, bias_in, g)
            back_spatial(g).start()

        @pl.when(is_temporal)
        def _():
            temporal_all(g)
            for r in range(1, 8):
                back_temporal(g, r).start()
            back[me % half, :, group_cols(g, width)] = wg_ref[0, 0, held_rows(3), group_cols(g)]

    def attend_rest(g):
        @pl.when(is_spatial)
        def _():
            spatial_frame(0, bias_ref, g)

    round_values(2)
    attend_first(0)
    forward_last(3)
    attend_rest(0)
    for k in range(4):
        multiply(3, k)
    round_values(3)
    attend_first(1)
    attend_rest(1)

    @pl.when(is_temporal)
    def _():
        bias_copy().wait_send()

    for g in range(2):
        @pl.when(is_temporal)
        def _():
            back_spatial(g).wait_recv()

        for q in range(half):
            @pl.when(me != half + q)
            def _():
                back_came(g, q).wait_recv()

    for h in range(heads):
        ranks = [n for n in range(kept) if n <= h <= n + kept]
        blocks = [
            (p, back[:, :, pl.ds(p * HD, HD)].reshape(frame_rows, HD))
            for p in ranks + [kept + n for n in ranks]
        ]
        res = chosen_sum((heads + h) * heads, blocks)
        out_ref[:, :, pl.ds(h * HD, HD)] = res.reshape(half, quarter, HD)

    for g in range(2):
        @pl.when(is_spatial)
        def _():
            back_spatial(g).wait_send()

        @pl.when(is_temporal)
        def _():
            for r in range(1, 8):
                back_temporal(g, r).wait_send()

    for r in range(8):
        near_copy(r).wait_send()
        core_copy(r).wait_send()
        pass_copy(r).wait_send()
    for r in range(8):
        sum_copy(r).wait_send()
    for p in range(3):
        cast_copy(p).wait_send()
    for j in range(half):
        @pl.when(me != half + j)
        def _():
            to_temporal(j).wait_send()

        @pl.when(is_temporal)
        def _():
            to_spatial(j).wait_send()

    for c in range(1, 4):
        sent_w(c)


def attend_block(masks, x_quarters, w_qkv, gains, bias, seq_count, fsdp_count):
    half, quarter, feats = x_quarters.shape
    kinds, rows, _ = w_qkv.shape
    cols = gains.shape[-1]
    dma = pltpu.SemaphoreType.DMA
    near = pl.BlockSpec(memory_space=pltpu.VMEM)
    sent = jnp.bfloat16
    lanes = -(-quarter // 128) * 128
    sums = (seq_count, 2, 8, lanes)
    return pl.pallas_call(
        block_kernel,
        out_shape=jax.ShapeDtypeStruct((half, quarter, 2 * cols), sent),
        in_specs=[
            near,
            pl.BlockSpec(memory_space=pl.ANY),
            near,
            near,
            near,
        ],
        out_specs=near,
        scratch_shapes=[
            pltpu.VMEM((seq_count, quarter, feats * fsdp_count), sent),
            pltpu.VMEM((kinds, seq_count, rows, cols), sent),
            pltpu.VMEM((kinds, rows, cols), sent),
            pltpu.VMEM((kinds, rows, cols), sent),
            pltpu.VMEM((kinds, seq_count, quarter, cols), jnp.float32),
            pltpu.VMEM(sums, jnp.float32),
            pltpu.VMEM((4,) + sums, jnp.float32),
            pltpu.VMEM(sums, jnp.float32),
            pltpu.VMEM(bias.shape, jnp.float32),
            pltpu.VMEM((half, quarter, 2 * cols), sent),
        ]
        + [dma((8,))] * 8
        + [dma((3,))] * 2
        + [dma((kinds + 1,))] * 9
        + [dma((kinds + 1, 4)), dma((kinds + 1, 4)), dma((8,)), dma((8,)), dma((half,))]
        + [dma, dma, dma((2, 8)), dma((2, 8))],
        compiler_params=pltpu.CompilerParams(
            collective_id=0, has_side_effects=True, vmem_limit_bytes=61 * 1024 * 1024
        ),
    )(masks, x_quarters, w_qkv, gains, bias)


def split_shards(x_tokens, w_qkv, q_gain, k_gain, head_kind, block_live):
    seq_count = lax.axis_size("seq")
    half = seq_count // 2
    me = lax.axis_index("seq")
    is_spatial = me < half
    rows, feats = x_tokens.shape
    quarter = rows // half
    head_count = head_kind.shape[0]
    kept = head_count // 2
    all_heads = jnp.arange(head_count)
    kinds = (head_kind > 0).astype(jnp.int32)
    before = all_heads[None, :] < all_heads[:, None]
    tm_before = jnp.sum(jnp.where(before, kinds[None, :], 0), axis=1)
    place = jnp.where(kinds > 0, kept + tm_before, all_heads - tm_before)
    order = jnp.sum(
        jnp.where(place[None, :] == all_heads[:, None], all_heads[None, :], 0), axis=1
    )
    flip = jnp.where(is_spatial, 0, kept)
    slots = jnp.arange(head_count)
    wanted = jnp.where(slots[:, None] == (slots[None, :] + flip) % head_count, order[:, None], 0)
    ordered = jnp.sum(wanted, axis=0)
    mine = ordered[:kept, None] == all_heads[None, :]
    both_gains = jnp.stack([q_gain, k_gain]).reshape(2, 1, head_count, HD)
    gains = jnp.sum(jnp.where(mine[None, :, :, None], both_gains, 0.0), axis=2)
    live = block_live[0].astype(jnp.float32)
    chosen = order[:kept, None] == all_heads[None, :]
    live = jnp.sum(jnp.where(chosen[:, :, None, None], live[None], 0.0), axis=1)
    bias = jnp.repeat(jnp.where(live > 0, 0.0, -1e30), BLK, axis=2)
    bias = jnp.pad(bias, ((0, 0), (0, -bias.shape[1] % 8), (0, 0)))
    at_heads = jnp.concatenate([ordered, place])[:, None] == all_heads[None, :]
    masks = jnp.broadcast_to(
        at_heads.astype(jnp.bfloat16).reshape(-1, 1, 1), (at_heads.size, 16, HD)
    )
    done = attend_block(
        masks,
        x_tokens.reshape(half, quarter, feats),
        w_qkv,
        gains.reshape(2, 1, kept * HD),
        bias,
        seq_count,
        lax.axis_size("fsdp"),
    )
    return done.reshape(rows, head_count * HD)


def solution(mesh):
    placed = (
        P("seq", "fsdp"),
        P(None, "seq", "fsdp"),
        P("fsdp"),
        P("fsdp"),
        P("fsdp"),
        P("seq", "fsdp", None, None),
    )

    def chosen(x_tokens, w_qkv, q_gain, k_gain, head_kind, block_live):
        fits = (
            mesh.shape["seq"] == 8
            and head_kind.shape[0] == 10
            and block_live.shape[0] == 1
            and x_tokens.shape[1] * mesh.shape["fsdp"] == w_qkv.shape[1] * mesh.shape["seq"]
            and mesh.shape["fsdp"] == 4
        )
        body = split_shards if fits else shards
        return body(x_tokens, w_qkv, q_gain, k_gain, head_kind, block_live)

    return jax.shard_map(
        chosen, mesh=mesh, in_specs=placed, out_specs=P("seq", "fsdp"), check_vma=False
    )
```

```python
import math

import jax
import jax.numpy as jnp
from jax import lax
from jax.experimental import pallas as pl
from jax.experimental.pallas import tpu as pltpu
from jax.sharding import PartitionSpec as P

H = 40
HD = 128
BLK = 128


def softmax_rows(scores):
    row_max = jnp.max(scores, axis=-1, keepdims=True)
    expo = jnp.exp(scores - row_max)
    return (expo / jnp.sum(expo, axis=-1, keepdims=True)).astype(jnp.bfloat16)


def spatial_attend(queries, keys_n, values, live_blocks):
    score_scale = 1.0 / math.sqrt(HD)
    scores = (
        jnp.einsum("fqhd,fkhd->fhqk", queries, keys_n, preferred_element_type=jnp.float32)
        * score_scale
    )
    key_mask = jnp.repeat(jnp.repeat(live_blocks, BLK, axis=2), BLK, axis=3)
    scores = jnp.where(key_mask, scores, -1e30)
    sp_weights = softmax_rows(scores)
    return jnp.einsum(
        "fhqk,fkhd->fqhd", sp_weights, values, preferred_element_type=jnp.float32
    ).astype(jnp.bfloat16)


def temporal_attend(triple):
    queries, keys_n, values = triple
    frame_count, single, pos_count, col_width = queries.shape
    head_count = col_width // HD
    grid_shape = (frame_count, pos_count, head_count, HD)
    score_scale = 1.0 / math.sqrt(HD)
    scores = (
        jnp.einsum(
            "fphd,gphd->phfg",
            queries.reshape(grid_shape),
            keys_n.reshape(grid_shape),
            preferred_element_type=jnp.float32,
        )
        * score_scale
    )
    tm_weights = softmax_rows(scores)
    result = jnp.einsum(
        "phfg,gphd->fphd",
        tm_weights,
        values.reshape(grid_shape),
        preferred_element_type=jnp.float32,
    )
    return result.astype(jnp.bfloat16).reshape(frame_count, single, pos_count, col_width)


def shards(x_tokens, w_qkv, q_gain, k_gain, head_kind, block_live):
    full_tokens = lax.all_gather(x_tokens, "fsdp", axis=1, tiled=True)
    tok_rows = full_tokens.shape[0]
    col_width = w_qkv.shape[2]

    def add_rows(shard_rows):
        return jnp.dot(full_tokens, shard_rows, preferred_element_type=jnp.float32)

    q_raw = add_rows(lax.all_gather(w_qkv[0], "seq", axis=0, tiled=True))
    k_raw = add_rows(lax.all_gather(w_qkv[1], "seq", axis=0, tiled=True))
    v_raw = add_rows(lax.all_gather(w_qkv[2], "seq", axis=0, tiled=True))
    q_sq, k_sq = lax.psum((jnp.sum(q_raw * q_raw, axis=1), jnp.sum(k_raw * k_raw, axis=1)), "fsdp")
    total_cols = H * HD
    queries = (q_raw * lax.rsqrt(q_sq[:, None] / total_cols + 1e-06) * q_gain).astype(jnp.bfloat16)
    keys_n = (k_raw * lax.rsqrt(k_sq[:, None] / total_cols + 1e-06) * k_gain).astype(jnp.bfloat16)
    values = v_raw.astype(jnp.bfloat16)
    seq_count = lax.axis_size("seq")
    frames_dev = block_live.shape[0]
    positions = tok_rows // frames_dev
    per_device = positions // seq_count
    head_count = col_width // HD
    live_blocks = block_live > 0

    def to_blocks(columns):
        return columns.reshape(frames_dev, seq_count, per_device, col_width)

    relayed = temporal_attend(
        (
            lax.all_to_all(to_blocks(queries), "seq", split_axis=1, concat_axis=0, tiled=True),
            lax.all_to_all(to_blocks(keys_n), "seq", split_axis=1, concat_axis=0, tiled=True),
            lax.all_to_all(to_blocks(values), "seq", split_axis=1, concat_axis=0, tiled=True),
        )
    )
    returned = lax.all_to_all(relayed, "seq", split_axis=0, concat_axis=1, tiled=True).reshape(
        tok_rows, col_width
    )
    grid_shape = (frames_dev, positions, head_count, HD)
    spatial = spatial_attend(
        queries.reshape(grid_shape),
        keys_n.reshape(grid_shape),
        values.reshape(grid_shape),
        live_blocks,
    )
    is_temporal = jnp.repeat(head_kind > 0, HD)[None, :]
    return jnp.where(is_temporal, returned, spatial.reshape(tok_rows, col_width))

def block_kernel(
    mask_ref, x_ref, w_ref, gain_ref, bias_ref, out_ref,
    xg_ref, wg_ref, oth_ref, relay_ref, total, sq, sq_in, sq_out, bias_in, back,
    x_send, x_recv, near_send, near_recv, core_send, core_recv, pass_send, pass_recv,
    cast_send, cast_recv, mate_send, mate_recv, cross_send, relay_recv, fwd_send, a1_send, a1_recv,
    a2_send, a2_recv, y_send, y_recv, sum_send, sum_recv, local_sem, bias_send, bias_recv,
    back_send, back_recv,
):
    me, fs = lax.axis_index("seq"), lax.axis_index("fsdp")
    quarter, feats = x_ref.shape[1:]
    kinds, _, width = oth_ref.shape
    kept = width // HD
    half = 4
    z, y = me // 2, me % 2
    mate = (z + 1 - 2 * (z % 2)) * 2 + y
    side = z // 2
    a1 = (2 - side) * 2 + y
    a2 = (3 - 3 * side) * 2 + y
    other_y = z * 2 + 1 - y
    inner = (z == 1) | (z == 2)
    outer = (z == 0) | (z == 3)
    is_spatial = me < half
    is_temporal = me >= half
    sib = fs + 1 - 2 * (fs % 2)
    across = (fs + 2) % 4

    barrier = pltpu.get_barrier_semaphore()
    for r in range(1, 8):
        pl.semaphore_signal(
            barrier, inc=1, device_id=((me + r) % 8, fs), device_id_type=pl.DeviceIdType.MESH
        )
    for r in range(1, 4):
        pl.semaphore_signal(
            barrier, inc=1, device_id=(me, (fs + r) % 4), device_id_type=pl.DeviceIdType.MESH
        )
    pl.semaphore_wait(barrier, 10)

    def remote(src, dst, send, recv, seq, fsdp):
        return pltpu.make_async_remote_copy(
            src_ref=src, dst_ref=dst, send_sem=send, recv_sem=recv,
            device_id=(seq, fsdp), device_id_type=pl.DeviceIdType.MESH,
        )

    def x_cols(f):
        return pl.ds(pl.multiple_of(f * feats, 128), feats)

    def slot(r, f):
        return xg_ref.at[r, :, x_cols(f)]

    def to_temporal(j):
        target = half + j
        r = (me + 8 - target) % 8
        return remote(x_ref.at[j], slot(r, fs), x_send.at[j], x_recv.at[r], target, fs)

    def to_spatial(j):
        target = (me + half) % 8
        return remote(
            x_ref.at[j], slot(half + j, fs), x_send.at[half + j], x_recv.at[half + j], target, fs
        )

    def keep_spatial(j):
        return pltpu.make_async_copy(x_ref.at[j], slot(j, fs), local_sem.at[j])

    def keep_temporal():
        return pltpu.make_async_copy(x_ref.at[me % half], slot(0, fs), local_sem.at[0])

    for j in range(half):
        @pl.when(me != half + j)
        def _():
            to_temporal(j).start()

        @pl.when(is_temporal)
        def _():
            to_spatial(j).start()

        @pl.when(is_spatial)
        def _():
            keep_spatial(j).start()

    @pl.when(is_temporal)
    def _():
        keep_temporal().start()

    early = (kept + 1) // 2
    cut_at = early * HD
    parts = ((0, 0, width), (1, 0, width), (2, 0, cut_at), (2, cut_at, width - cut_at))

    def held(c, row):
        i, low, size = parts[c]
        return wg_ref.at[i, row, :, pl.ds(low, size)]

    def loose(ref, c):
        i, low, size = parts[c]
        return ref.at[i, :, pl.ds(low, size)]

    def mate_copy(c):
        return remote(held(c, me), held(c, me), mate_send.at[c], mate_recv.at[c], mate, fs)

    def relay_copy(c):
        return remote(
            loose(oth_ref, c), loose(relay_ref, c), cross_send.at[c], relay_recv.at[c], mate, fs
        )

    def cross_copy(c):
        return remote(loose(oth_ref, c), held(c, me), cross_send.at[c], a1_recv.at[c], a1, fs)

    def fwd_copy(c):
        return remote(loose(relay_ref, c), held(c, mate), fwd_send.at[c], a2_recv.at[c], a1, fs)

    def a1_copy(c):
        return remote(held(c, a1), held(c, a1), a1_send.at[c], a1_recv.at[c], mate, fs)

    def a2_copy(c):
        return remote(held(c, a2), held(c, a2), a2_send.at[c], a2_recv.at[c], mate, fs)

    def y_copy(c, k):
        at = held(c, (me, mate, a1, a2)[k])
        return remote(at, at, y_send.at[c, k], y_recv.at[c, k], other_y, fs)

    heads = 2 * kept

    def chosen_sum(first, blocks):
        found = None
        for h, block in blocks:
            rows = block.shape[0] // mask_ref.shape[1]
            term = block.reshape(rows, *mask_ref.shape[1:]) * mask_ref[first + h][None]
            found = term if found is None else found + term
        return found.reshape(-1, HD)

    def pick_w(i):
        def cut(h):
            return w_ref[i, :, pl.ds(h * HD, HD)]

        for n in range(kept):
            near_heads = range(n, n + kept + 1)
            to = pl.ds(n * HD, HD)
            wg_ref[i, me, :, to] = chosen_sum(n * heads, [(h, cut(h)) for h in near_heads])
            oth_ref[i, :, to] = chosen_sum((kept + n) * heads, [(h, cut(h)) for h in near_heads])

    def start_w(i):
        mate_copy(i).start()

        @pl.when(outer)
        def _():
            relay_copy(i).start()

        @pl.when(inner)
        def _():
            cross_copy(i).start()

        y_copy(i, 0).start()

    def forward_w(i):
        mate_copy(i).wait_recv()
        y_copy(i, 1).start()

        @pl.when(inner)
        def _():
            relay_copy(i).wait_recv()
            fwd_copy(i).start()

        a1_copy(i).wait_recv()

        @pl.when(inner)
        def _():
            a1_copy(i).start()

        y_copy(i, 2).start()

    def forward_last(i):
        a2_copy(i).wait_recv()

        @pl.when(inner)
        def _():
            a2_copy(i).start()

        y_copy(i, 3).start()

    pick_w(0)
    start_w(0)
    pick_w(1)
    start_w(1)
    pick_w(2)

    def bias_copy():
        return remote(bias_ref, bias_in, bias_send, bias_recv, (me + half) % 8, fs)

    @pl.when(is_temporal)
    def _():
        bias_copy().start()

    def near_copy(r):
        return remote(slot(r, fs), slot(r, fs), near_send.at[r], near_recv.at[r], me, across)

    def core_copy(r):
        return remote(slot(r, fs), slot(r, fs), core_send.at[r], core_recv.at[r], me, sib)

    def pass_copy(r):
        at = slot(r, across)
        return remote(at, at, pass_send.at[r], pass_recv.at[r], me, sib)

    def x_arrived(r):
        remote(x_ref.at[0], slot(r, fs), x_send.at[0], x_recv.at[r], me, across).wait_recv()

    for r in range(8):
        if r == 0:
            @pl.when(is_temporal)
            def _():
                keep_temporal().wait()
        else:
            @pl.when(is_temporal)
            def _():
                x_arrived(r)
        if r < half:
            @pl.when(is_spatial)
            def _():
                keep_spatial(r).wait()
        else:
            @pl.when(is_spatial)
            def _():
                x_arrived(r)
        near_copy(r).start()
        core_copy(r).start()

    forward_w(0)
    forward_w(1)
    start_w(2)
    start_w(3)

    for r in range(8):
        remote(
            slot(r, across), slot(r, across), near_send.at[r], near_recv.at[r], me, across
        ).wait_recv()
        pass_copy(r).start()

    forward_last(0)
    forward_last(1)

    for r in range(8):
        core_copy(r).wait_recv()
        pass_copy(r).wait_recv()

    def multiply(c, k):
        i, low, size = parts[c]
        y_copy(c, k).wait_recv()
        at_z = ((me, mate, a1, a2)[k]) // 2
        cols = pl.ds(pl.multiple_of(at_z * feats, 128), feats)
        to = pl.ds(low, size)

        def rows(t, carry):
            at = pl.ds(t * half, half)
            left = xg_ref[at, :, cols].reshape(half * quarter, feats)
            right = wg_ref[i, pl.ds(at_z * 2, 2), :, to].reshape(feats, size)
            term = jnp.dot(left, right, preferred_element_type=jnp.float32)
            term = term.reshape(half, quarter, size)
            if k == 0:
                total[i, at, :, to] = term
            else:
                total[i, at, :, to] = total[i, at, :, to] + term
            return carry

        lax.fori_loop(0, 2, rows, 0)

    def sent_w(c):
        mate_copy(c).wait_send()
        cross_copy(c).wait_send()

        @pl.when(inner)
        def _():
            fwd_copy(c).wait_send()
            a1_copy(c).wait_send()
            a2_copy(c).wait_send()

        for k in range(4):
            y_copy(c, k).wait_send()

    multiply(0, 0)
    multiply(1, 0)
    forward_w(2)
    for k in range(1, 3):
        multiply(0, k)
        multiply(1, k)
    multiply(0, 3)
    multiply(1, 3)

    ones = jnp.ones((8, wg_ref.shape[3]), jnp.bfloat16)
    last = (((1,), (1,)), ((), ()))

    def sum_slot(r, carry):
        for i in range(2):
            raw = total[i, r]
            square = raw * raw
            high = square.astype(jnp.bfloat16)
            low = (square - high.astype(jnp.float32)).astype(jnp.bfloat16)
            found = lax.dot_general(ones, high, last, preferred_element_type=jnp.float32)
            found = found + lax.dot_general(ones, low, last, preferred_element_type=jnp.float32)
            sq[r, i] = jnp.concatenate(
                [found, jnp.zeros((8, sq.shape[3] - quarter), jnp.float32)], axis=1
            )
        return carry

    lax.fori_loop(0, 8, sum_slot, 0)

    def cast_copy(p):
        return remote(sq, sq_in.at[p], cast_send.at[p], cast_recv.at[p], me, (fs + p + 1) % 4)

    for p in range(3):
        cast_copy(p).start()
    forward_last(2)
    forward_w(3)
    for k in range(2):
        multiply(2, k)
    for p in range(3):
        cast_copy(p).wait_recv()
    sq_out[...] = (sq[...] + sq_in[0]) + (sq_in[1] + sq_in[2])

    def sum_copy(r):
        frame_sp = me + r // half * half
        part = r % half
        to_t = half + part
        at_t = (frame_sp + 2 * 8 - to_t) % 8
        frame_tm = (me + r) % 8
        to_s = frame_tm % half
        at_s = frame_tm // half * half + me % half
        target = jnp.where(is_spatial, to_t, to_s)
        at = jnp.where(is_spatial, at_t, at_s)
        return remote(sq_out.at[r], sq_in.at[3, at], sum_send.at[r], sum_recv.at[at], target, fs)

    def sum_came(r):
        return remote(sq_out.at[r], sq_in.at[3, r], sum_send.at[r], sum_recv.at[r], (me + 1) % 8, fs)

    for r in range(8):
        sum_copy(r).start()
    for k in range(2, 4):
        multiply(2, k)
    for r in range(8):
        sum_came(r).wait_recv()

    sent_w(0)

    def held_rows(i):
        return pl.ds(i * quarter, quarter)

    def norm_slot(r, carry):
        for i in range(2):
            whole = sq_out[r, i] + sq_in[3, r, i]
            scale = lax.rsqrt(whole / (H * HD) + 1e-06)
            scale = jnp.transpose(scale)[:quarter, :1]
            normed = (total[i, r] * scale * gain_ref[i]).astype(jnp.bfloat16)
            wg_ref[0, r, held_rows(i)] = normed
        return carry

    lax.fori_loop(0, 8, norm_slot, 0)

    def round_values(c):
        _, low, size = parts[c]

        def value_slot(r, carry):
            found = total[2, r, :, pl.ds(low, size)]
            wg_ref[0, r, held_rows(2), pl.ds(low, size)] = found.astype(jnp.bfloat16)
            return carry

        lax.fori_loop(0, 8, value_slot, 0)

    factor = math.log2(math.e) / math.sqrt(HD)

    def head_cols(h):
        return pl.ds(pl.multiple_of(h * HD, HD), HD)

    group_heads = ((0, early), (early, kept))

    def group_cols(g, first=0):
        low, high = group_heads[g]
        return pl.ds(first + low * HD, (high - low) * HD)

    def weigh(scores, vals):
        row_max = jnp.max(scores, axis=-1, keepdims=True)
        expo = jnp.exp2(scores - row_max)
        inverse = 1.0 / jnp.sum(expo, axis=-1, keepdims=True)
        mixed = jnp.dot(expo.astype(jnp.bfloat16), vals, preferred_element_type=jnp.float32)
        return (mixed * inverse).astype(jnp.bfloat16)

    frame_rows = half * quarter

    def spatial_frame(frame, mask_ref, g):
        at = pl.ds(frame * half, half)

        def one_head(h, carry):
            qs, ks, vs = [
                wg_ref[0, at, held_rows(i), head_cols(h)].reshape(frame_rows, HD)
                for i in range(3)
            ]
            pieces = []
            for qb in range(frame_rows // BLK):
                scores = lax.dot_general(
                    qs[qb * BLK : (qb + 1) * BLK], ks, last, preferred_element_type=jnp.float32
                )
                pieces.append(weigh(scores * factor + mask_ref[h, pl.ds(qb, 1)], vs))
            res = jnp.concatenate(pieces, axis=0).reshape(half, quarter, HD)
            if frame == 0:
                back[:, :, head_cols(h)] = res
            else:
                wg_ref[0, at, held_rows(3), head_cols(h)] = res
            return carry

        lax.fori_loop(*group_heads[g], one_head, 0)

    step = 32
    mix = 8 * step

    def temporal_all(g):
        row_pos = lax.broadcasted_iota(jnp.int32, (mix, mix), 0) % step
        col_pos = lax.broadcasted_iota(jnp.int32, (mix, mix), 1) % step
        hide = jnp.where(row_pos == col_pos, 0.0, -1e30)

        def one_head(h, carry):
            for pb in range(quarter // step):
                qs, ks, vs = [
                    wg_ref[0, :, pl.ds(i * quarter + pb * step, step), head_cols(h)].reshape(mix, HD)
                    for i in range(3)
                ]
                scores = lax.dot_general(qs, ks, last, preferred_element_type=jnp.float32)
                res = weigh(scores * factor + hide, vs)
                to = pl.ds(3 * quarter + pb * step, step)
                wg_ref[0, :, to, head_cols(h)] = res.reshape(8, step, HD)
            return carry

        lax.fori_loop(*group_heads[g], one_head, 0)

    def back_spatial(g):
        return remote(
            wg_ref.at[0, pl.ds(half, half), held_rows(3), group_cols(g)],
            back.at[:, :, group_cols(g)],
            back_send.at[g, 0], back_recv.at[g, 0], (me + half) % 8, fs,
        )

    def back_temporal(g, r):
        return remote(
            wg_ref.at[0, r, held_rows(3), group_cols(g)],
            back.at[me % half, :, group_cols(g, width)],
            back_send.at[g, r], back_recv.at[g, 1 + me % half], (me + r) % 8, fs,
        )

    def back_came(g, q):
        return remote(
            wg_ref.at[0, 0, held_rows(3), group_cols(g)],
            back.at[q, :, group_cols(g, width)],
            back_send.at[g, 0], back_recv.at[g, 1 + q], (me + 1) % 8, fs,
        )

    def attend_first(g):
        @pl.when(is_spatial)
        def _():
            if g == 0:
                bias_copy().wait_recv()
            spatial_frame(1, bias_in, g)
            back_spatial(g).start()

        @pl.when(is_temporal)
        def _():
            temporal_all(g)
            for r in range(1, 8):
                back_temporal(g, r).start()
            back[me % half, :, group_cols(g, width)] = wg_ref[0, 0, held_rows(3), group_cols(g)]

    def attend_rest(g):
        @pl.when(is_spatial)
        def _():
            spatial_frame(0, bias_ref, g)

    round_values(2)
    attend_first(0)
    forward_last(3)
    attend_rest(0)
    for k in range(4):
        multiply(3, k)
    round_values(3)
    attend_first(1)
    attend_rest(1)

    @pl.when(is_temporal)
    def _():
        bias_copy().wait_send()

    for g in range(2):
        @pl.when(is_temporal)
        def _():
            back_spatial(g).wait_recv()

        for q in range(half):
            @pl.when(me != half + q)
            def _():
                back_came(g, q).wait_recv()

    for h in range(heads):
        ranks = [n for n in range(kept) if n <= h <= n + kept]
        blocks = [
            (p, back[:, :, pl.ds(p * HD, HD)].reshape(frame_rows, HD))
            for p in ranks + [kept + n for n in ranks]
        ]
        res = chosen_sum((heads + h) * heads, blocks)
        out_ref[:, :, pl.ds(h * HD, HD)] = res.reshape(half, quarter, HD)

    for g in range(2):
        @pl.when(is_spatial)
        def _():
            back_spatial(g).wait_send()

        @pl.when(is_temporal)
        def _():
            for r in range(1, 8):
                back_temporal(g, r).wait_send()

    for r in range(8):
        near_copy(r).wait_send()
        core_copy(r).wait_send()
        pass_copy(r).wait_send()
    for r in range(8):
        sum_copy(r).wait_send()
    for p in range(3):
        cast_copy(p).wait_send()
    for j in range(half):
        @pl.when(me != half + j)
        def _():
            to_temporal(j).wait_send()

        @pl.when(is_temporal)
        def _():
            to_spatial(j).wait_send()

    for c in range(1, 4):
        sent_w(c)


def attend_block(masks, x_quarters, w_qkv, gains, bias, seq_count, fsdp_count):
    half, quarter, feats = x_quarters.shape
    kinds, rows, _ = w_qkv.shape
    cols = gains.shape[-1]
    dma = pltpu.SemaphoreType.DMA
    near = pl.BlockSpec(memory_space=pltpu.VMEM)
    sent = jnp.bfloat16
    lanes = -(-quarter // 128) * 128
    sums = (seq_count, 2, 8, lanes)
    return pl.pallas_call(
        block_kernel,
        out_shape=jax.ShapeDtypeStruct((half, quarter, 2 * cols), sent),
        in_specs=[
            near,
            pl.BlockSpec(memory_space=pl.ANY),
            near,
            near,
            near,
        ],
        out_specs=near,
        scratch_shapes=[
            pltpu.VMEM((seq_count, quarter, feats * fsdp_count), sent),
            pltpu.VMEM((kinds, seq_count, rows, cols), sent),
            pltpu.VMEM((kinds, rows, cols), sent),
            pltpu.VMEM((kinds, rows, cols), sent),
            pltpu.VMEM((kinds, seq_count, quarter, cols), jnp.float32),
            pltpu.VMEM(sums, jnp.float32),
            pltpu.VMEM((4,) + sums, jnp.float32),
            pltpu.VMEM(sums, jnp.float32),
            pltpu.VMEM(bias.shape, jnp.float32),
            pltpu.VMEM((half, quarter, 2 * cols), sent),
        ]
        + [dma((8,))] * 8
        + [dma((3,))] * 2
        + [dma((kinds + 1,))] * 9
        + [dma((kinds + 1, 4)), dma((kinds + 1, 4)), dma((8,)), dma((8,)), dma((half,))]
        + [dma, dma, dma((2, 8)), dma((2, 8))],
        compiler_params=pltpu.CompilerParams(
            collective_id=0, has_side_effects=True, vmem_limit_bytes=61 * 1024 * 1024
        ),
    )(masks, x_quarters, w_qkv, gains, bias)


def split_shards(x_tokens, w_qkv, q_gain, k_gain, head_kind, block_live):
    seq_count = lax.axis_size("seq")
    half = seq_count // 2
    me = lax.axis_index("seq")
    is_spatial = me < half
    rows, feats = x_tokens.shape
    quarter = rows // half
    head_count = head_kind.shape[0]
    kept = head_count // 2
    all_heads = jnp.arange(head_count)
    kinds = (head_kind > 0).astype(jnp.int32)
    before = all_heads[None, :] < all_heads[:, None]
    tm_before = jnp.sum(jnp.where(before, kinds[None, :], 0), axis=1)
    place = jnp.where(kinds > 0, kept + tm_before, all_heads - tm_before)
    order = jnp.sum(
        jnp.where(place[None, :] == all_heads[:, None], all_heads[None, :], 0), axis=1
    )
    flip = jnp.where(is_spatial, 0, kept)
    slots = jnp.arange(head_count)
    wanted = jnp.where(slots[:, None] == (slots[None, :] + flip) % head_count, order[:, None], 0)
    ordered = jnp.sum(wanted, axis=0)
    mine = ordered[:kept, None] == all_heads[None, :]
    both_gains = jnp.stack([q_gain, k_gain]).reshape(2, 1, head_count, HD)
    gains = jnp.sum(jnp.where(mine[None, :, :, None], both_gains, 0.0), axis=2)
    live = block_live[0].astype(jnp.float32)
    chosen = order[:kept, None] == all_heads[None, :]
    live = jnp.sum(jnp.where(chosen[:, :, None, None], live[None], 0.0), axis=1)
    bias = jnp.repeat(jnp.where(live > 0, 0.0, -1e30), BLK, axis=2)
    bias = jnp.pad(bias, ((0, 0), (0, -bias.shape[1] % 8), (0, 0)))
    at_heads = jnp.concatenate([ordered, place])[:, None] == all_heads[None, :]
    masks = jnp.broadcast_to(
        at_heads.astype(jnp.bfloat16).reshape(-1, 1, 1), (at_heads.size, 16, HD)
    )
    done = attend_block(
        masks,
        x_tokens.reshape(half, quarter, feats),
        w_qkv,
        gains.reshape(2, 1, kept * HD),
        bias,
        seq_count,
        lax.axis_size("fsdp"),
    )
    return done.reshape(rows, head_count * HD)


def solution(mesh):
    placed = (
        P("seq", "fsdp"),
        P(None, "seq", "fsdp"),
        P("fsdp"),
        P("fsdp"),
        P("fsdp"),
        P("seq", "fsdp", None, None),
    )

    def chosen(x_tokens, w_qkv, q_gain, k_gain, head_kind, block_live):
        fits = (
            mesh.shape["seq"] == 8
            and head_kind.shape[0] == 10
            and block_live.shape[0] == 1
            and x_tokens.shape[1] * mesh.shape["fsdp"] == w_qkv.shape[1] * mesh.shape["seq"]
            and mesh.shape["fsdp"] == 4
        )
        body = split_shards if fits else shards
        return body(x_tokens, w_qkv, q_gain, k_gain, head_kind, block_live)

    return jax.shard_map(
        chosen, mesh=mesh, in_specs=placed, out_specs=P("seq", "fsdp"), check_vma=False
    )
```
